256 devices in a mesh: cuts: 64 (over y_lo, z, x), dom: 4 (over y_hi, core).
Axes of the slice: x: 4, y: 4 (y_hi: 2, y_lo: 2; y = y_hi * 2 + y_lo), z: 8, core: 2. Of those that a mesh axis runs over, the one named last changes fastest.
Arguments:
- particles: float32 [2, 5, 64, 65536], P(None, None, 'cuts', 'dom'), may hold values from -5 to 5, as said below
- cells: int32 [2, 64, 65536], P(None, 'cuts', 'dom'), may hold values from 0 to 16383
- counts: int32 [2, 2, 64, 4], P(None, None, 'cuts', 'dom'), may hold values from 0 to 4096, as said below
Outputs:
- kept: float32 [2, 5, 64, 65536], P(None, None, 'cuts', 'dom')
- arrivals: float32 [2, 5, 64, 32768], P(None, None, 'cuts', 'dom')
The draws below stay inside these ranges and needn't reach their ends.
Inputs may be any that keep to these rules, and one draw needn't show every extreme that they name: `particles`: components 0 to 3 are coordinates; component 4 is a positive weight between 0.25 and 4. `counts`: each count is at most 4096, and some count equals 4096.
All inputs are finite; a program needn't handle non-finite values.
Results may differ from the reference program's by a relative error of at most 0.00025.
Values sent between devices are 32-bit elements; how exact they have to be, the bound alone decides.
A program may use at most 64 MiB of HBM per device.

```python
import math
import jax
import jax.numpy as jnp
from jax import lax

GRID = 128
PARTICLES = 16384
SECTIONS = 3
CAPACITY = 4096
SLICES = 64
DOMAINS = 4
PART_SLICE = 65536


def draw_particles(key, part):
    key = jax.random.fold_in(key, 11)
    key_coord, key_weight = jax.random.split(key)
    coord_shape = (2, 4, SLICES, PART_SLICE)
    weight_shape = (2, 1, SLICES, PART_SLICE)
    coords = jnp.clip(jax.random.normal(key_coord, coord_shape, jnp.float32), -5.0, 5.0)
    weights = jnp.exp(jax.random.uniform(key_weight, weight_shape, jnp.float32, math.log(0.5), math.log(2.0)))
    return jnp.concatenate([coords, weights], axis=1)


def draw_counts(key, part):
    key = jax.random.fold_in(key, 23)
    key_count, key_peak = jax.random.split(key)
    values = jax.random.randint(key_count, (2, 2, SLICES, DOMAINS), 0, CAPACITY + 1)
    flattened = values.reshape(-1)
    peak_spot = jax.random.randint(key_peak, (), 0, flattened.shape[0])
    flattened = jnp.where(jnp.arange(flattened.shape[0]) == peak_spot, CAPACITY, flattened)
    return flattened.reshape(2, 2, SLICES, DOMAINS).astype(jnp.int32)


def set_ends(result, key, least, largest):
    dims = result.shape
    spot = [jax.random.randint(jax.random.fold_in(key, axis), (), 0, dims[axis]) for axis in range(len(dims))]
    result = result.at[tuple(spot)].set(least)
    longest = dims.index(max(dims))
    spot[longest] = (spot[longest] + 1) % dims[longest]
    return result.at[tuple(spot)].set(largest)


def setup_inputs(seed: int = 0) -> dict:
    splits = jax.random.split(jax.random.key(seed), 4)
    return {
        "particles": draw_particles(jax.random.fold_in(splits[3], 71), 0),
        "cells": set_ends(jax.random.randint(splits[1], (2, SLICES, PART_SLICE), 0, GRID * GRID), jax.random.fold_in(splits[1], 1), 0, (GRID * GRID) - 1).astype(jnp.int32),
        "counts": draw_counts(jax.random.fold_in(splits[3], 71), 0),
    }


KICK_SCALE = 0.01
ADJUST_X = 0.31
ADJUST_Y = 0.32

def sine_basis(grid_size):
    index = jnp.arange(grid_size, dtype=jnp.int32) + 1
    product = index[:, None] * index[None, :] % (2 * (grid_size + 1))
    angle = product.astype(jnp.float32) * (math.pi / (grid_size + 1))
    basis = math.sqrt(2.0 / (grid_size + 1)) * jnp.sin(angle)
    eigen = 2.0 - 2.0 * jnp.cos(index.astype(jnp.float32) * (math.pi / (grid_size + 1)))
    return (basis, eigen[:, None] + eigen[None, :])

def solve_fields(density, basis, eigen_sum):
    highest = lax.Precision.HIGHEST
    spectrum = jnp.dot(jnp.dot(basis, density, precision=highest, preferred_element_type=jnp.float32), basis, precision=highest, preferred_element_type=jnp.float32)
    inner = jnp.dot(basis, spectrum / eigen_sum, precision=highest, preferred_element_type=jnp.float32)
    potential = jnp.dot(inner, basis, precision=highest, preferred_element_type=jnp.float32)
    padded = jnp.pad(potential, 1)
    field_x = (padded[:-2, 1:-1] - padded[2:, 1:-1]) * 0.5
    field_y = (padded[1:-1, :-2] - padded[1:-1, 2:]) * 0.5
    return (field_x, field_y)

def deposit_one(cell_row, weight_row):
    return jnp.zeros((GRID * GRID,), weight_row.dtype).at[cell_row].add(weight_row)

def reference(particles, cells, counts):
    weights = particles[:, 4]
    density = jax.vmap(jax.vmap(deposit_one))(cells, weights).reshape(2, SLICES, GRID, GRID)
    basis, eigen_sum = sine_basis(GRID)
    solver = jax.vmap(jax.vmap(lambda grid_one: solve_fields(grid_one, basis, eigen_sum)))
    field_x, field_y = solver(density)
    field_x = field_x.reshape(2, SLICES, GRID * GRID)
    field_y = field_y.reshape(2, SLICES, GRID * GRID)
    mom_x = [particles[0, 1], particles[1, 1]]
    mom_y = [particles[0, 3], particles[1, 3]]
    for section_num in range(1, SECTIONS + 1):
        ahead_x = jnp.roll(field_x[1], -section_num, axis=0)
        ahead_y = jnp.roll(field_y[1], -section_num, axis=0)
        behind_x = jnp.roll(field_x[0], section_num, axis=0)
        behind_y = jnp.roll(field_y[0], section_num, axis=0)
        mom_x[0] = mom_x[0] + KICK_SCALE * jnp.take_along_axis(ahead_x, cells[0], axis=1)
        mom_y[0] = mom_y[0] + KICK_SCALE * jnp.take_along_axis(ahead_y, cells[0], axis=1)
        mom_x[1] = mom_x[1] + KICK_SCALE * jnp.take_along_axis(behind_x, cells[1], axis=1)
        mom_y[1] = mom_y[1] + KICK_SCALE * jnp.take_along_axis(behind_y, cells[1], axis=1)
    cos_x, sin_x = (math.cos(2 * math.pi * ADJUST_X), math.sin(2 * math.pi * ADJUST_X))
    cos_y, sin_y = (math.cos(2 * math.pi * ADJUST_Y), math.sin(2 * math.pi * ADJUST_Y))
    beams_out = []
    for beam_no in range(2):
        pos_x = particles[beam_no, 0]
        pos_y = particles[beam_no, 2]
        new_x = cos_x * pos_x + sin_x * mom_x[beam_no]
        new_px = -sin_x * pos_x + cos_x * mom_x[beam_no]
        new_y = cos_y * pos_y + sin_y * mom_y[beam_no]
        new_py = -sin_y * pos_y + cos_y * mom_y[beam_no]
        beams_out.append(jnp.stack([new_x, new_px, new_y, new_py, particles[beam_no, 4]], axis=0))
    final_state = jnp.stack(beams_out, axis=0).reshape(2, 5, SLICES, DOMAINS, PARTICLES)
    up_count = counts[:, 0][:, None, :, :, None]
    down_count = counts[:, 1][:, None, :, :, None]
    slot_index = jnp.arange(PARTICLES, dtype=jnp.int32)
    leaving = (slot_index >= PARTICLES - up_count) | (slot_index < down_count)
    kept_state = jnp.where(leaving, 0.0, final_state).reshape(2, 5, SLICES, PART_SLICE)
    block_slot = jnp.arange(CAPACITY, dtype=jnp.int32)
    up_block = jnp.where(block_slot < up_count, final_state[..., PARTICLES - CAPACITY:][..., ::-1], 0.0)
    down_block = jnp.where(block_slot < down_count, final_state[..., :CAPACITY], 0.0)
    zero_slice = jnp.zeros_like(up_block[:, :, :1])
    from_below = jnp.concatenate([zero_slice, up_block[:, :, :-1]], axis=2)
    from_above = jnp.concatenate([down_block[:, :, 1:], zero_slice], axis=2)
    arrivals = jnp.concatenate([from_below, from_above], axis=-1).reshape(2, 5, SLICES, DOMAINS * 2 * CAPACITY)
    return (kept_state, arrivals)
```

```python
import functools
import math

import jax
import jax.numpy as jnp
import numpy as np
from jax import lax
from jax.experimental import pallas as pl
from jax.experimental.pallas import tpu as pltpu
from jax.sharding import PartitionSpec as P

MESH = pl.DeviceIdType.MESH
GRID = 128
SECTIONS = 3
ROWS = 128
BLOCK = 32
KICK_SCALE = 0.01
COS_X, SIN_X = (math.cos(2 * math.pi * 0.31), math.sin(2 * math.pi * 0.31))
COS_Y, SIN_Y = (math.cos(2 * math.pi * 0.32), math.sin(2 * math.pi * 0.32))
F32, BF16 = jnp.float32, jnp.bfloat16
PEERS = ((0, 1), (1, 0), (1, 1))


def constants():
    index = np.arange(1, GRID + 1)
    angle = (index[:, None] * index[None, :] % (2 * (GRID + 1))) * (np.pi / (GRID + 1))
    basis = math.sqrt(2.0 / (GRID + 1)) * np.sin(angle)
    padded = np.pad(basis, ((1, 1), (0, 0)))
    slope = (padded[:-2] - padded[2:]) * (0.5 * KICK_SCALE)
    eigen = 2.0 - 2.0 * np.cos(index * (np.pi / (GRID + 1)))
    inverse = 1.0 / (eigen[:, None] + eigen[None, :])
    return np.stack([basis, slope, inverse, slope.T]).astype(np.float32)


def dot(a, b):
    return jnp.dot(a, b, precision=lax.Precision.HIGHEST, preferred_element_type=F32)


def across(row):
    return jnp.broadcast_to(row, (GRID, 128))


def deposit(cells, weights, levels):
    row = (cells >> 7).astype(F32).astype(BF16)
    column = (cells & 127).astype(F32).astype(BF16)
    high = weights.astype(BF16)
    low = (weights - high.astype(F32)).astype(BF16)
    zero, one = jnp.zeros((GRID, 128), BF16), jnp.ones((GRID, 128), BF16)
    hit_column, part_high, part_low = [], [], []
    for i in range(cells.shape[0]):
        here = levels == across(row[i : i + 1])
        part_high.append(jnp.where(here, across(high[i : i + 1]), zero))
        part_low.append(jnp.where(here, across(low[i : i + 1]), zero))
        hit_column.append(jnp.where(levels == across(column[i : i + 1]), one, zero))
    left = jnp.concatenate(
        [jnp.concatenate(part_high, axis=1), jnp.concatenate(part_low, axis=1)], axis=0
    )
    right = jnp.concatenate(hit_column, axis=1)
    both = lax.dot_general(left, right, (((1,), (1,)), ((), ())), preferred_element_type=F32)
    return both[:GRID] + both[GRID:]


def lookup(cells, field, levels, row_levels):
    row = cells >> 7
    column = (cells & 127).astype(F32).astype(BF16)
    zero, one = jnp.zeros((GRID, 128), BF16), jnp.ones((GRID, 128), BF16)
    hit = jnp.concatenate(
        [jnp.where(levels == across(column[i : i + 1]), one, zero) for i in range(cells.shape[0])],
        axis=1,
    )
    picked = jnp.dot(field, jnp.concatenate([hit, hit], axis=0), preferred_element_type=F32)
    value_x, value_y = [], []
    for i in range(cells.shape[0]):
        here = row_levels == across(row[i : i + 1])
        lanes = slice(128 * i, 128 * (i + 1))
        value_x.append(jnp.sum(jnp.where(here, picked[:GRID, lanes], 0.0), axis=0, keepdims=True))
        value_y.append(jnp.sum(jnp.where(here, picked[GRID:, lanes], 0.0), axis=0, keepdims=True))
    return jnp.concatenate(value_x, axis=0), jnp.concatenate(value_y, axis=0)


def reversed_block(block):
    lanes = 127 - lax.broadcasted_iota(jnp.int32, (8, 128), 1)
    rows = 7 - lax.broadcasted_iota(jnp.int32, (8, 128), 0)
    pieces = []
    for i in reversed(range(block.shape[0] // 8)):
        piece = jnp.take_along_axis(block[8 * i : 8 * i + 8], lanes, axis=1)
        pieces.append(jnp.take_along_axis(piece, rows, axis=0))
    return jnp.concatenate(pieces, axis=0)


def turn(state):
    pos_x, mom_x, pos_y, mom_y = state
    return (
        COS_X * pos_x + SIN_X * mom_x,
        -SIN_X * pos_x + COS_X * mom_x,
        COS_Y * pos_y + SIN_Y * mom_y,
        -SIN_Y * pos_y + COS_Y * mom_y,
    )


def kicked(base, kick_x, kick_y):
    return (
        base[0] + SIN_X * kick_x,
        base[1] + COS_X * kick_x,
        base[2] + SIN_Y * kick_y,
        base[3] + COS_Y * kick_y,
    )


def kernel(
    slices,
    particles,
    cells,
    counts,
    table,
    kept,
    arrivals,
    state,
    cell,
    const,
    grid,
    pair_in,
    half,
    window_in,
    spectrum,
    field,
    out_state,
    leavers,
    leaver_kicks,
    arrived,
    arrived_kicks,
    in_sem,
    out_sem,
    pair_sem,
    window_sem,
    quarter_sem,
    leave_sem,
    kick_sem,
):
    me = lax.axis_index("cuts")
    dom = lax.axis_index("dom")
    y_hi, core = dom // 2, dom % 2

    def behind(distance):
        return lax.rem(me + (distance + slices), slices)

    def member(y_flip, core_flip):
        y = 1 - y_hi if y_flip else y_hi
        c = 1 - core if core_flip else core
        return y * 2 + c

    def send(src, dst, sems, index, cut, member_no):
        copy = pltpu.make_async_remote_copy(
            src_ref=src,
            dst_ref=dst,
            send_sem=sems.at[(0, *index)],
            recv_sem=sems.at[(1, *index)],
            device_id=(cut, member_no),
            device_id_type=MESH,
        )
        copy.start()
        return copy

    loads = {}
    for beam in (1, 0):
        loads["cells", beam] = pltpu.make_async_copy(
            cells.at[beam], cell.at[beam], in_sem.at[beam]
        )
        loads["weights", beam] = pltpu.make_async_copy(
            particles.at[beam, 4], state.at[beam, 4], in_sem.at[2 + beam]
        )
    for beam in (0, 1):
        loads["coords", beam] = pltpu.make_async_copy(
            particles.at[beam, pl.ds(0, 4)], state.at[beam, pl.ds(0, 4)], in_sem.at[4 + beam]
        )
    loads["table"] = pltpu.make_async_copy(table, const, in_sem.at[6])
    for load in loads.values():
        load.start()

    barrier = pltpu.get_barrier_semaphore()
    partners = [(me, member(*flips)) for flips in PEERS]
    for distance in range(1, SECTIONS + 1):
        for sign in (1, -1):
            for y_flip in (0, 1):
                partners.append((behind(sign * distance), member(y_flip, 0)))
    for partner in partners:
        pl.semaphore_signal(barrier, inc=1, device_id=partner, device_id_type=MESH)

    levels = lax.broadcasted_iota(jnp.int32, (GRID, 128), 0).astype(F32).astype(BF16)
    row_levels = lax.broadcasted_iota(jnp.int32, (GRID, 128), 0)
    copies = []

    def deposit_rows(beam, first, count, step):
        def some(i, total):
            rows = pl.ds(pl.multiple_of(first + i * step, step), step)
            return total + deposit(cell[beam, rows, :], state[beam, 4, rows, :], levels)

        return lax.fori_loop(0, count // step, some, jnp.zeros((GRID, GRID), F32))

    def pair_send(beam):
        other = pl.ds(pl.multiple_of((1 - core) * 64, 64), 64)
        copy = send(grid.at[beam, other], pair_in.at[beam], pair_sem, (beam,), me, member(0, 1))
        copies.append(copy)
        return copy

    def window_send(beam, pair_copy):
        pair_copy.wait_recv()
        mine = pl.ds(pl.multiple_of(core * 64, 64), 64)
        half[beam] = grid[beam, mine, :] + pair_in[beam]
        sent = []
        for distance in (1, 3, 2):
            for y_flip in (1, 0):
                y = 1 - y_hi if y_flip else y_hi
                rows = pl.ds(pl.multiple_of(y * BLOCK, BLOCK), BLOCK)
                cut = behind(-distance if beam == 1 else distance)
                sent.append(
                    send(
                        half.at[beam, rows],
                        window_in.at[beam, distance - 1, y_flip],
                        window_sem,
                        (beam, distance - 1, y_flip),
                        cut,
                        member(y_flip, 0),
                    )
                )
        copies.extend(sent)
        return sent

    def quarter_send(beam, window_copies):
        for copy in window_copies:
            copy.wait_recv()
        quarter = window_in[beam, 0, 0]
        for distance in range(SECTIONS):
            for y_flip in (0, 1):
                if distance or y_flip:
                    quarter = quarter + window_in[beam, distance, y_flip]
        rows = pl.ds(pl.multiple_of(core * 64 + y_hi * BLOCK, BLOCK), BLOCK)
        spectrum[beam, rows, :] = dot(quarter, const[0])
        sent = []
        for number, flips in enumerate(PEERS):
            place = spectrum.at[beam, rows]
            sent.append(send(place, place, quarter_sem, (beam, number), me, member(*flips)))
        copies.extend(sent)
        return sent

    def solve(beam, quarter_copies):
        for copy in quarter_copies:
            copy.wait_recv()
        basis, slope, inverse, slope_t = const[0], const[1], const[2], const[3]
        scaled = dot(basis, spectrum[beam]) * inverse
        both = dot(jnp.concatenate([slope, basis], axis=0), scaled)
        field_x = dot(both[:GRID], basis)
        field_y = dot(both[GRID:], slope_t)
        fields = jnp.concatenate([field_x, field_y], axis=0)
        high = fields.astype(BF16)
        low = (fields - high.astype(F32)).astype(BF16)
        field[beam] = jnp.concatenate([high, low], axis=1)

    row_place = lax.broadcasted_iota(jnp.int32, (BLOCK, 128), 0) * 128 + lax.broadcasted_iota(
        jnp.int32, (BLOCK, 128), 1
    )
    up_count = [jnp.where(me == slices - 1, 0, counts[beam, 0, 0, 0]) for beam in range(2)]
    down_count = [jnp.where(me == 0, 0, counts[beam, 1, 0, 0]) for beam in range(2)]

    def leave_send(beam):
        loads["coords", beam].wait()
        for way in range(2):
            rows = slice(ROWS - BLOCK, ROWS) if way == 0 else slice(0, BLOCK)
            limit = (up_count if way == 0 else down_count)[beam]
            base = turn([state[beam, comp, rows, :] for comp in range(4)])
            for comp, value in enumerate((*base, state[beam, 4, rows, :])):
                if way == 0:
                    value = reversed_block(value)
                leavers[way, beam, comp] = jnp.where(row_place < limit, value, 0.0)
            copies.append(
                send(
                    leavers.at[way, beam],
                    arrived.at[beam, :, pl.ds(way * BLOCK, BLOCK)],
                    leave_sem,
                    (way, beam),
                    behind(1 if way == 0 else -1),
                    dom,
                )
            )
        return copies[-2:]

    def look_up_block(beam, block):
        rows = pl.ds(pl.multiple_of(block * BLOCK, BLOCK), BLOCK)
        kick_x, kick_y = lookup(cell[beam, rows, :], field[1 - beam], levels, row_levels)
        place = row_place + block * (BLOCK * 128)
        stays = (place < ROWS * 128 - counts[beam, 0, 0, 0]) & (place >= counts[beam, 1, 0, 0])
        base = turn([state[beam, comp, rows, :] for comp in range(4)])
        for comp, value in enumerate(
            (*kicked(base, kick_x, kick_y), state[beam, 4, rows, :])
        ):
            out_state[beam, comp, rows, :] = jnp.where(stays, value, 0.0)
        return kick_x, kick_y

    def look_up(beam):
        sent = []
        def end(i, _):
            kick_x, kick_y = look_up_block(beam, i * 3)
            rows = pl.ds(pl.multiple_of(i * BLOCK, BLOCK), BLOCK)
            leaver_kicks[beam, 0, rows, :] = kick_x
            leaver_kicks[beam, 1, rows, :] = kick_y
            return 0

        lax.fori_loop(0, 2, end, 0)
        for comp in range(2):
            up = reversed_block(leaver_kicks[beam, comp, BLOCK:, :])
            leaver_kicks[beam, comp, BLOCK:, :] = jnp.where(row_place < up_count[beam], up, 0.0)
            down = leaver_kicks[beam, comp, :BLOCK, :]
            leaver_kicks[beam, comp, :BLOCK, :] = jnp.where(row_place < down_count[beam], down, 0.0)
        for way in range(2):
            sent.append(
                send(
                    leaver_kicks.at[beam, :, pl.ds((1 - way) * BLOCK, BLOCK)],
                    arrived_kicks.at[beam, :, pl.ds(way * BLOCK, BLOCK)],
                    kick_sem,
                    (way, beam),
                    behind(1 if way == 0 else -1),
                    dom,
                )
            )
        copies.extend(sent)

        def middle(i, _):
            look_up_block(beam, i + 1)
            return 0

        lax.fori_loop(0, 2, middle, 0)
        store = pltpu.make_async_copy(out_state.at[beam], kept.at[beam], out_sem.at[beam])
        store.start()
        return sent, store

    def arrive(beam, leave_copies, kick_copies):
        for copy in (*leave_copies, *kick_copies):
            copy.wait_recv()
        base = [arrived[beam, comp] for comp in range(4)]
        done = kicked(base, arrived_kicks[beam, 0], arrived_kicks[beam, 1])
        for comp in range(4):
            arrived[beam, comp] = done[comp]
        store = pltpu.make_async_copy(arrived.at[beam], arrivals.at[beam], out_sem.at[2 + beam])
        store.start()
        return store

    loads["cells", 1].wait()
    loads["weights", 1].wait()
    grid[1] = deposit_rows(1, 0, ROWS, 32)
    pl.semaphore_wait(barrier, len(partners))
    pair_1 = pair_send(1)
    loads["cells", 0].wait()
    loads["weights", 0].wait()
    first = deposit_rows(0, 0, ROWS // 2, 32)
    window_1 = window_send(1, pair_1)
    grid[0] = first + deposit_rows(0, ROWS // 2, ROWS // 2, 32)
    pair_0 = pair_send(0)
    loads["table"].wait()
    window_0 = window_send(0, pair_0)
    quarter_1 = quarter_send(1, window_1)
    leave_0 = leave_send(0)
    leave_1 = leave_send(1)
    quarter_0 = quarter_send(0, window_0)
    solve(1, quarter_1)
    kicks_0, store_0 = look_up(0)
    solve(0, quarter_0)
    kicks_1, store_1 = look_up(1)
    stores = [store_0, store_1]
    stores.append(arrive(0, leave_0, kicks_0))
    stores.append(arrive(1, leave_1, kicks_1))
    for copy in copies:
        copy.wait_send()
    for store in stores:
        store.wait()


def local(slices, particles, cells, counts):
    anywhere = pl.BlockSpec(memory_space=pl.ANY)
    dma = pltpu.SemaphoreType.DMA
    kept, arrivals = pl.pallas_call(
        functools.partial(kernel, slices),
        out_shape=(
            jax.ShapeDtypeStruct((2, 5, ROWS, 128), F32),
            jax.ShapeDtypeStruct((2, 5, 2 * BLOCK, 128), F32),
        ),
        in_specs=[
            anywhere,
            anywhere,
            pl.BlockSpec(memory_space=pltpu.SMEM),
            anywhere,
        ],
        out_specs=(anywhere, anywhere),
        scratch_shapes=[
            pltpu.VMEM((2, 5, ROWS, 128), F32),
            pltpu.VMEM((2, ROWS, 128), jnp.int32),
            pltpu.VMEM((4, GRID, GRID), F32),
            pltpu.VMEM((2, GRID, GRID), F32),
            pltpu.VMEM((2, GRID // 2, GRID), F32),
            pltpu.VMEM((2, GRID // 2, GRID), F32),
            pltpu.VMEM((2, SECTIONS, 2, BLOCK, GRID), F32),
            pltpu.VMEM((2, GRID, GRID), F32),
            pltpu.VMEM((2, 2 * GRID, 2 * GRID), BF16),
            pltpu.VMEM((2, 5, ROWS, 128), F32),
            pltpu.VMEM((2, 2, 5, BLOCK, 128), F32),
            pltpu.VMEM((2, 2, 2 * BLOCK, 128), F32),
            pltpu.VMEM((2, 5, 2 * BLOCK, 128), F32),
            pltpu.VMEM((2, 2, 2 * BLOCK, 128), F32),
            dma((7,)),
            dma((4,)),
            dma((2, 2)),
            dma((2, 2, SECTIONS, 2)),
            dma((2, 2, 3)),
            dma((2, 2, 2)),
            dma((2, 2, 2)),
        ],
        compiler_params=pltpu.CompilerParams(
            collective_id=0, has_side_effects=True, vmem_limit_bytes=56 * 2**20
        ),
        cost_estimate=pl.CostEstimate(
            flops=7 * 10**9, bytes_accessed=2 * 10**6, transcendentals=0
        ),
        name="crossing",
    )(
        particles.reshape(2, 5, ROWS, 128),
        cells.reshape(2, ROWS, 128),
        counts,
        jnp.asarray(constants()),
    )
    return kept.reshape(2, 5, 1, ROWS * 128), arrivals.reshape(2, 5, 1, 2 * BLOCK * 128)


def solution(mesh):
    return jax.shard_map(
        functools.partial(local, mesh.shape["cuts"]),
        mesh=mesh,
        in_specs=(
            P(None, None, "cuts", "dom"),
            P(None, "cuts", "dom"),
            P(None, None, "cuts", "dom"),
        ),
        out_specs=(P(None, None, "cuts", "dom"), P(None, None, "cuts", "dom")),
        check_vma=False,
    )
```

```python
import functools
import math

import jax
import jax.numpy as jnp
import numpy as np
from jax import lax
from jax.experimental import pallas as pl
from jax.experimental.pallas import tpu as pltpu
from jax.sharding import PartitionSpec as P

MESH = pl.DeviceIdType.MESH
GRID = 128
SECTIONS = 3
ROWS = 128
BLOCK = 32
KICK_SCALE = 0.01
COS_X, SIN_X = (math.cos(2 * math.pi * 0.31), math.sin(2 * math.pi * 0.31))
COS_Y, SIN_Y = (math.cos(2 * math.pi * 0.32), math.sin(2 * math.pi * 0.32))
F32, BF16 = jnp.float32, jnp.bfloat16


def constants():
    index = np.arange(1, GRID + 1)
    angle = (index[:, None] * index[None, :] % (2 * (GRID + 1))) * (np.pi / (GRID + 1))
    basis = math.sqrt(2.0 / (GRID + 1)) * np.sin(angle)
    padded = np.pad(basis, ((1, 1), (0, 0)))
    slope = (padded[:-2] - padded[2:]) * (0.5 * KICK_SCALE)
    eigen = 2.0 - 2.0 * np.cos(index * (np.pi / (GRID + 1)))
    inverse = 1.0 / (eigen[:, None] + eigen[None, :])
    return np.stack([basis, slope, inverse, slope.T]).astype(np.float32)


def dot(a, b):
    return jnp.dot(a, b, precision=lax.Precision.HIGHEST, preferred_element_type=F32)


def across(row):
    return jnp.broadcast_to(row, (GRID, 128))


def deposit(cells, weights, levels):
    row = (cells >> 7).astype(F32).astype(BF16)
    column = (cells & 127).astype(F32).astype(BF16)
    high = weights.astype(BF16)
    low = (weights - high.astype(F32)).astype(BF16)
    zero, one = jnp.zeros((GRID, 128), BF16), jnp.ones((GRID, 128), BF16)
    hit_column, part_high, part_low = [], [], []
    for i in range(cells.shape[0]):
        here = levels == across(row[i : i + 1])
        part_high.append(jnp.where(here, across(high[i : i + 1]), zero))
        part_low.append(jnp.where(here, across(low[i : i + 1]), zero))
        hit_column.append(jnp.where(levels == across(column[i : i + 1]), one, zero))
    left = jnp.concatenate(
        [jnp.concatenate(part_high, axis=1), jnp.concatenate(part_low, axis=1)], axis=0
    )
    right = jnp.concatenate(hit_column, axis=1)
    both = lax.dot_general(left, right, (((1,), (1,)), ((), ())), preferred_element_type=F32)
    return both[:GRID] + both[GRID:]


def lookup(cells, field, levels, row_levels):
    row = cells >> 7
    column = (cells & 127).astype(F32).astype(BF16)
    zero, one = jnp.zeros((GRID, 128), BF16), jnp.ones((GRID, 128), BF16)
    hit = jnp.concatenate(
        [jnp.where(levels == across(column[i : i + 1]), one, zero) for i in range(cells.shape[0])],
        axis=1,
    )
    picked = jnp.dot(field, jnp.concatenate([hit, hit], axis=0), preferred_element_type=F32)
    value_x, value_y = [], []
    for i in range(cells.shape[0]):
        here = row_levels == across(row[i : i + 1])
        lanes = slice(128 * i, 128 * (i + 1))
        value_x.append(jnp.sum(jnp.where(here, picked[:GRID, lanes], 0.0), axis=0, keepdims=True))
        value_y.append(jnp.sum(jnp.where(here, picked[GRID:, lanes], 0.0), axis=0, keepdims=True))
    return jnp.concatenate(value_x, axis=0), jnp.concatenate(value_y, axis=0)


def reversed_block(block):
    lanes = 127 - lax.broadcasted_iota(jnp.int32, (8, 128), 1)
    rows = 7 - lax.broadcasted_iota(jnp.int32, (8, 128), 0)
    pieces = []
    for i in reversed(range(block.shape[0] // 8)):
        piece = jnp.take_along_axis(block[8 * i : 8 * i + 8], lanes, axis=1)
        pieces.append(jnp.take_along_axis(piece, rows, axis=0))
    return jnp.concatenate(pieces, axis=0)


def turn(state):
    pos_x, mom_x, pos_y, mom_y = state
    return (
        COS_X * pos_x + SIN_X * mom_x,
        -SIN_X * pos_x + COS_X * mom_x,
        COS_Y * pos_y + SIN_Y * mom_y,
        -SIN_Y * pos_y + COS_Y * mom_y,
    )


def kicked(base, kick_x, kick_y):
    return (
        base[0] + SIN_X * kick_x,
        base[1] + COS_X * kick_x,
        base[2] + SIN_Y * kick_y,
        base[3] + COS_Y * kick_y,
    )


def kernel(
    slices,
    particles,
    cells,
    counts_in,
    table,
    kept,
    arrivals,
    state,
    cell,
    const,
    counts,
    grid,
    pair_in,
    half,
    window_in,
    spectrum,
    field,
    leavers,
    leaver_kicks,
    arrived,
    arrived_kicks,
    in_sem,
    pair_sem,
    window_sem,
    share_sem,
    leave_sem,
    kick_sem,
):
    me = lax.axis_index("cuts")
    dom = lax.axis_index("dom")
    y_hi, core = dom // 2, dom % 2

    def behind(distance):
        return lax.rem(me + (distance + slices), slices)

    def member(y_flip, core_flip):
        y = 1 - y_hi if y_flip else y_hi
        c = 1 - core if core_flip else core
        return y * 2 + c

    def send(src, dst, sems, index, cut, member_no):
        copy = pltpu.make_async_remote_copy(
            src_ref=src,
            dst_ref=dst,
            send_sem=sems.at[(0, *index)],
            recv_sem=sems.at[(1, *index)],
            device_id=(cut, member_no),
            device_id_type=MESH,
        )
        copy.start()
        return copy

    loads = {}
    for beam in (0, 1):
        loads["cells", beam] = pltpu.make_async_copy(
            cells.at[beam], cell.at[beam], in_sem.at[beam]
        )
        loads["weights", beam] = pltpu.make_async_copy(
            particles.at[beam, 4], state.at[beam, 4], in_sem.at[2 + beam]
        )
    for beam in (0, 1):
        loads["coords", beam] = pltpu.make_async_copy(
            particles.at[beam, pl.ds(0, 4)], state.at[beam, pl.ds(0, 4)], in_sem.at[4 + beam]
        )
    loads["table"] = pltpu.make_async_copy(table, const, in_sem.at[6])
    loads["counts"] = pltpu.make_async_copy(counts_in, counts, in_sem.at[7])
    for load in loads.values():
        load.start()

    barrier = pltpu.get_barrier_semaphore()
    partners = [(me, member(0, 1))]
    for distance in range(1, SECTIONS + 1):
        for sign in (1, -1):
            for y_flip in (0, 1):
                partners.append((behind(sign * distance), member(y_flip, 0)))
    for partner in partners:
        pl.semaphore_signal(barrier, inc=1, device_id=partner, device_id_type=MESH)

    levels = lax.broadcasted_iota(jnp.int32, (GRID, 128), 0).astype(F32).astype(BF16)
    row_levels = lax.broadcasted_iota(jnp.int32, (GRID, 128), 0)
    copies = []

    def deposit_rows(beam, first, count, step):
        def some(i, total):
            rows = pl.ds(pl.multiple_of(first + i * step, step), step)
            return total + deposit(cell[beam, rows, :], state[beam, 4, rows, :], levels)

        return lax.fori_loop(0, count // step, some, jnp.zeros((GRID, GRID), F32))

    def pair_send(beam):
        other = pl.ds(pl.multiple_of((1 - core) * 64, 64), 64)
        copy = send(grid.at[beam, other], pair_in.at[beam], pair_sem, (beam,), me, member(0, 1))
        copies.append(copy)
        return copy

    def window_send(beam, pair_copy):
        pair_copy.wait_recv()
        mine = pl.ds(pl.multiple_of(core * 64, 64), 64)
        half[beam] = grid[beam, mine, :] + pair_in[beam]
        sent = []
        for distance in (2, 3, 1):
            for y_flip in (1, 0):
                cut = behind(-distance if beam == 1 else distance)
                sent.append(
                    send(
                        half.at[beam],
                        window_in.at[beam, distance - 1, y_flip],
                        window_sem,
                        (beam, distance - 1, y_flip),
                        cut,
                        member(y_flip, 0),
                    )
                )
        copies.extend(sent)
        return sent

    def share(beam, window_copies):
        for copy in window_copies:
            copy.wait_recv()
        total = window_in[beam, 0, 0]
        for distance in range(SECTIONS):
            for y_flip in (0, 1):
                if distance or y_flip:
                    total = total + window_in[beam, distance, y_flip]
        rows = pl.ds(pl.multiple_of(core * 64, 64), 64)
        spectrum[beam, rows, :] = dot(total, const[0])
        place = spectrum.at[beam, rows]
        copy = send(place, place, share_sem, (beam,), me, member(0, 1))
        copies.append(copy)
        return copy

    def solve(beam, share_copy):
        share_copy.wait_recv()
        basis, slope, inverse, slope_t = const[0], const[1], const[2], const[3]
        scaled = dot(basis, spectrum[beam]) * inverse
        both = dot(jnp.concatenate([slope, basis], axis=0), scaled)
        field_x = dot(both[:GRID], basis)
        field_y = dot(both[GRID:], slope_t)
        fields = jnp.concatenate([field_x, field_y], axis=0)
        high = fields.astype(BF16)
        low = (fields - high.astype(F32)).astype(BF16)
        field[beam] = jnp.concatenate([high, low], axis=1)

    row_place = lax.broadcasted_iota(jnp.int32, (BLOCK, 128), 0) * 128 + lax.broadcasted_iota(
        jnp.int32, (BLOCK, 128), 1
    )
    def leave_pack(beam):
        loads["coords", beam].wait()
        for way in range(2):
            rows = slice(ROWS - BLOCK, ROWS) if way == 0 else slice(0, BLOCK)
            limit = (up_count if way == 0 else down_count)[beam]
            base = turn([state[beam, comp, rows, :] for comp in range(4)])
            for comp, value in enumerate((*base, state[beam, 4, rows, :])):
                if way == 0:
                    value = reversed_block(value)
                leavers[way, beam, comp] = jnp.where(row_place < limit, value, 0.0)

    def leave_send(beam):
        for way in range(2):
            copies.append(
                send(
                    leavers.at[way, beam],
                    arrived.at[beam, :, pl.ds(way * BLOCK, BLOCK)],
                    leave_sem,
                    (way, beam),
                    behind(1 if way == 0 else -1),
                    dom,
                )
            )
        return copies[-2:]

    def look_up_block(beam, block):
        rows = pl.ds(pl.multiple_of(block * BLOCK, BLOCK), BLOCK)
        kick_x, kick_y = lookup(cell[beam, rows, :], field[1 - beam], levels, row_levels)
        place = row_place + block * (BLOCK * 128)
        stays = (place < ROWS * 128 - counts[beam, 0, 0, 0]) & (place >= counts[beam, 0, 0, 1])
        base = turn([state[beam, comp, rows, :] for comp in range(4)])
        for comp, value in enumerate(
            (*kicked(base, kick_x, kick_y), state[beam, 4, rows, :])
        ):
            kept[beam, comp, rows, :] = jnp.where(stays, value, 0.0)
        return kick_x, kick_y

    def look_up_end(beam, end):
        kick_x, kick_y = look_up_block(beam, end * 3)
        rows = slice(end * BLOCK, (end + 1) * BLOCK)
        limit = (down_count if end == 0 else up_count)[beam]
        for comp, kick in enumerate((kick_x, kick_y)):
            if end == 1:
                kick = reversed_block(kick)
            leaver_kicks[beam, comp, rows, :] = jnp.where(row_place < limit, kick, 0.0)
        way = 1 - end
        copy = send(
            leaver_kicks.at[beam, :, pl.ds(end * BLOCK, BLOCK)],
            arrived_kicks.at[beam, :, pl.ds(way * BLOCK, BLOCK)],
            kick_sem,
            (way, beam),
            behind(1 if way == 0 else -1),
            dom,
        )
        copies.append(copy)
        return copy

    def look_up_middle(beam):
        def middle(i, _):
            look_up_block(beam, i + 1)
            return 0

        lax.fori_loop(0, 2, middle, 0)

    def arrive(beam, leave_copies, kick_copies):
        for copy in (*leave_copies, *kick_copies):
            copy.wait_recv()
        base = [arrived[beam, comp] for comp in range(4)]
        done = kicked(base, arrived_kicks[beam, 0], arrived_kicks[beam, 1])
        for comp, value in enumerate((*done, arrived[beam, 4])):
            arrivals[beam, comp] = value

    loads["cells", 0].wait()
    loads["weights", 0].wait()
    grid[0] = deposit_rows(0, 0, ROWS, ROWS)
    pl.semaphore_wait(barrier, len(partners))
    pair_0 = pair_send(0)
    loads["cells", 1].wait()
    loads["weights", 1].wait()
    first = deposit_rows(1, 0, ROWS // 2, ROWS // 2)
    window_0 = window_send(0, pair_0)
    grid[1] = first + deposit_rows(1, ROWS // 2, ROWS // 2, ROWS // 2)
    pair_1 = pair_send(1)
    loads["counts"].wait()
    up_count = [jnp.where(me == slices - 1, 0, counts[beam, 0, 0, 0]) for beam in range(2)]
    down_count = [jnp.where(me == 0, 0, counts[beam, 0, 0, 1]) for beam in range(2)]
    for beam in range(2):
        leave_pack(beam)
    window_1 = window_send(1, pair_1)
    leave = [leave_send(beam) for beam in range(2)]
    loads["table"].wait()
    share_0 = share(0, window_0)
    solve(0, share_0)
    kicks_1 = [look_up_end(1, 0)]
    share_1 = share(1, window_1)
    kicks_1.append(look_up_end(1, 1))
    solve(1, share_1)
    kicks_0 = [look_up_end(0, 0), look_up_end(0, 1)]
    look_up_middle(1)
    look_up_middle(0)
    arrive(1, leave[1], kicks_1)
    arrive(0, leave[0], kicks_0)
    for copy in copies:
        copy.wait_send()


def store_kernel(kept_in, arrivals_in, kept, arrivals, sems):
    stores = [
        pltpu.make_async_copy(kept_in, kept, sems.at[0]),
        pltpu.make_async_copy(arrivals_in, arrivals, sems.at[1]),
    ]
    for store in stores:
        store.start()
    for store in stores:
        store.wait()


def local(slices, particles, cells, counts):
    in_hbm = pl.BlockSpec(memory_space=pltpu.HBM)
    dma = pltpu.SemaphoreType.DMA
    in_vmem = pl.BlockSpec(memory_space=pltpu.VMEM)
    shapes = (
        jax.ShapeDtypeStruct((2, 5, ROWS, 128), F32),
        jax.ShapeDtypeStruct((2, 5, 2 * BLOCK, 128), F32),
    )
    results = pl.pallas_call(
        functools.partial(kernel, slices),
        out_shape=shapes,
        in_specs=[
            in_hbm,
            in_hbm,
            in_hbm,
            in_hbm,
        ],
        out_specs=(in_vmem, in_vmem),
        scratch_shapes=[
            pltpu.VMEM((2, 5, ROWS, 128), F32),
            pltpu.VMEM((2, ROWS, 128), jnp.int32),
            pltpu.VMEM((4, GRID, GRID), F32),
            pltpu.SMEM((2, 1, 1, 2), jnp.int32),
            pltpu.VMEM((2, GRID, GRID), F32),
            pltpu.VMEM((2, GRID // 2, GRID), F32),
            pltpu.VMEM((2, GRID // 2, GRID), F32),
            pltpu.VMEM((2, SECTIONS, 2, GRID // 2, GRID), F32),
            pltpu.VMEM((2, GRID, GRID), F32),
            pltpu.VMEM((2, 2 * GRID, 2 * GRID), BF16),
            pltpu.VMEM((2, 2, 5, BLOCK, 128), F32),
            pltpu.VMEM((2, 2, 2 * BLOCK, 128), F32),
            pltpu.VMEM((2, 5, 2 * BLOCK, 128), F32),
            pltpu.VMEM((2, 2, 2 * BLOCK, 128), F32),
            dma((8,)),
            dma((2, 2)),
            dma((2, 2, SECTIONS, 2)),
            dma((2, 2)),
            dma((2, 2, 2)),
            dma((2, 2, 2)),
        ],
        compiler_params=pltpu.CompilerParams(
            collective_id=0, has_side_effects=True, vmem_limit_bytes=40 * 2**20
        ),
        cost_estimate=pl.CostEstimate(
            flops=7 * 10**9, bytes_accessed=2 * 10**6, transcendentals=0
        ),
        name="crossing",
    )(
        pltpu.with_memory_space_constraint(particles.reshape(2, 5, ROWS, 128), pltpu.HBM),
        pltpu.with_memory_space_constraint(cells.reshape(2, ROWS, 128), pltpu.HBM),
        pltpu.with_memory_space_constraint(counts.transpose(0, 2, 3, 1), pltpu.HBM),
        pltpu.with_memory_space_constraint(jnp.asarray(constants()), pltpu.HBM),
    )
    kept, arrivals = pl.pallas_call(
        store_kernel,
        out_shape=shapes,
        in_specs=[in_vmem, in_vmem],
        out_specs=(in_hbm, in_hbm),
        scratch_shapes=[dma((2,))],
        name="store",
    )(*results)
    return kept.reshape(2, 5, 1, ROWS * 128), arrivals.reshape(2, 5, 1, 2 * BLOCK * 128)


def solution(mesh):
    return jax.shard_map(
        functools.partial(local, mesh.shape["cuts"]),
        mesh=mesh,
        in_specs=(
            P(None, None, "cuts", "dom"),
            P(None, "cuts", "dom"),
            P(None, None, "cuts", "dom"),
        ),
        out_specs=(P(None, None, "cuts", "dom"), P(None, None, "cuts", "dom")),
        check_vma=False,
    )
```

```python
import functools
import math

import jax
import jax.numpy as jnp
import numpy as np
from jax import lax
from jax.experimental import pallas as pl
from jax.experimental.pallas import tpu as pltpu
from jax.sharding import PartitionSpec as P

MESH = pl.DeviceIdType.MESH
GRID = 128
SECTIONS = 3
ROWS = 128
BLOCK = 32
DEPOSIT_ROWS = 64
LOOK_ROWS = 32
KICK_SCALE = 0.01
COS_X, SIN_X = (math.cos(2 * math.pi * 0.31), math.sin(2 * math.pi * 0.31))
COS_Y, SIN_Y = (math.cos(2 * math.pi * 0.32), math.sin(2 * math.pi * 0.32))
F32, BF16 = jnp.float32, jnp.bfloat16


def parts(values):
    high = values.astype(BF16)
    return high, (values - high.astype(F32)).astype(BF16)


def left_factor(a):
    high, low = parts(a)
    return jnp.concatenate([high, high, low], axis=1)


def right_factor(b):
    high, low = parts(b)
    return jnp.concatenate([high, low, high], axis=0)


def constants():
    index = np.arange(1, GRID + 1)
    angle = (index[:, None] * index[None, :] % (2 * (GRID + 1))) * (np.pi / (GRID + 1))
    basis = math.sqrt(2.0 / (GRID + 1)) * np.sin(angle)
    padded = np.pad(basis, ((1, 1), (0, 0)))
    slope = (padded[:-2] - padded[2:]) * (0.5 * KICK_SCALE)
    eigen = 2.0 - 2.0 * np.cos(index * (np.pi / (GRID + 1)))
    inverse = 1.0 / (eigen[:, None] + eigen[None, :])
    order = np.concatenate([np.arange(0, GRID, 2), np.arange(1, GRID, 2)])
    return np.stack([basis, slope[order], basis[order], slope.T, inverse]).astype(np.float32)


def times_const(a, right):
    return jnp.dot(left_factor(a), right, preferred_element_type=F32)


def const_times(left, b):
    return jnp.dot(left, right_factor(b), preferred_element_type=F32)


def across(row):
    return jnp.broadcast_to(row, (GRID, 128))


def deposit(cells, weights, levels):
    row = (cells >> 7).astype(F32).astype(BF16)
    column = (cells & 127).astype(F32).astype(BF16)
    high, low = parts(weights)
    zero, one = jnp.zeros((GRID, 128), BF16), jnp.ones((GRID, 128), BF16)
    hit_column, part_high, part_low = [], [], []
    for i in range(cells.shape[0]):
        here = levels == across(row[i : i + 1])
        part_high.append(jnp.where(here, across(high[i : i + 1]), zero))
        part_low.append(jnp.where(here, across(low[i : i + 1]), zero))
        hit_column.append(jnp.where(levels == across(column[i : i + 1]), one, zero))
    left = jnp.concatenate(
        [jnp.concatenate(part_high, axis=1), jnp.concatenate(part_low, axis=1)], axis=0
    )
    right = jnp.concatenate(hit_column, axis=1)
    both = lax.dot_general(left, right, (((1,), (1,)), ((), ())), preferred_element_type=F32)
    return both[:GRID] + both[GRID:]


def lookup(cells, field, levels, row_levels):
    pair = cells >> 8
    place = (cells & 255).astype(F32).astype(BF16)
    zero, one = jnp.zeros((2 * GRID, 128), BF16), jnp.ones((2 * GRID, 128), BF16)
    half = GRID // 2
    value_x, value_y = [], []
    for first in range(0, cells.shape[0], 2):
        hits = [
            jnp.where(levels == jnp.broadcast_to(place[i : i + 1], (2 * GRID, 128)), one, zero)
            for i in (first, first + 1)
        ]
        picked = jnp.dot(field, jnp.concatenate(hits, axis=1), preferred_element_type=F32)
        for i in (0, 1):
            here = row_levels == jnp.broadcast_to(pair[first + i : first + i + 1], (half, 128))
            part = picked[:, 128 * i : 128 * (i + 1)]
            both_x = part[:half] + part[GRID : GRID + half]
            both_y = part[half:GRID] + part[GRID + half :]
            value_x.append(jnp.sum(jnp.where(here, both_x, 0.0), axis=0, keepdims=True))
            value_y.append(jnp.sum(jnp.where(here, both_y, 0.0), axis=0, keepdims=True))
    return jnp.concatenate(value_x, axis=0), jnp.concatenate(value_y, axis=0)


def reversed_block(block):
    lanes = 127 - lax.broadcasted_iota(jnp.int32, (8, 128), 1)
    rows = 7 - lax.broadcasted_iota(jnp.int32, (8, 128), 0)
    pieces = []
    for i in reversed(range(block.shape[0] // 8)):
        piece = jnp.take_along_axis(block[8 * i : 8 * i + 8], lanes, axis=1)
        pieces.append(jnp.take_along_axis(piece, rows, axis=0))
    return jnp.concatenate(pieces, axis=0)


def turn(state):
    pos_x, mom_x, pos_y, mom_y = state
    return (
        COS_X * pos_x + SIN_X * mom_x,
        -SIN_X * pos_x + COS_X * mom_x,
        COS_Y * pos_y + SIN_Y * mom_y,
        -SIN_Y * pos_y + COS_Y * mom_y,
    )


def kicked(base, kick_x, kick_y):
    return (
        base[0] + SIN_X * kick_x,
        base[1] + COS_X * kick_x,
        base[2] + SIN_Y * kick_y,
        base[3] + COS_Y * kick_y,
    )


def kernel(
    slices,
    particles,
    cells,
    counts_in,
    table,
    kept,
    arrived,
    arrived_kicks,
    state,
    cell,
    const,
    lefts,
    rights,
    counts,
    grid,
    pair_in,
    half,
    window_in,
    spectrum,
    field,
    leavers,
    kicks,
    leaver_kicks,
    in_sem,
    pair_sem,
    window_sem,
    share_sem,
    leave_sem,
    kick_sem,
):
    me = lax.axis_index("cuts")
    dom = lax.axis_index("dom")
    y_hi, core = dom // 2, dom % 2

    def behind(distance):
        return lax.rem(me + (distance + slices), slices)

    def member(y_flip, core_flip):
        y = 1 - y_hi if y_flip else y_hi
        c = 1 - core if core_flip else core
        return y * 2 + c

    def remote(src, dst, sems, index, cut, member_no):
        copy = pltpu.make_async_remote_copy(
            src_ref=src,
            dst_ref=dst,
            send_sem=sems.at[(0, *index)],
            recv_sem=sems.at[(1, *index)],
            device_id=(cut, member_no),
            device_id_type=MESH,
        )
        return copy

    loads = {}
    for beam in (0, 1):
        loads["cells", beam] = pltpu.make_async_copy(
            cells.at[beam], cell.at[beam], in_sem.at[beam]
        )
        loads["weights", beam] = pltpu.make_async_copy(
            particles.at[beam, 4], state.at[beam, 4], in_sem.at[2 + beam]
        )
    for beam in (0, 1):
        loads["coords", beam] = pltpu.make_async_copy(
            particles.at[beam, pl.ds(0, 4)], state.at[beam, pl.ds(0, 4)], in_sem.at[4 + beam]
        )
    loads["table"] = pltpu.make_async_copy(table, const, in_sem.at[6])
    loads["counts"] = pltpu.make_async_copy(counts_in, counts, in_sem.at[7])
    for load in loads.values():
        load.start()

    barrier = pltpu.get_barrier_semaphore()
    partners = [(me, member(0, 1))]
    for distance in range(1, SECTIONS + 1):
        for sign in (1, -1):
            for y_flip in (0, 1):
                partners.append((behind(sign * distance), member(y_flip, 0)))
    for partner in partners:
        pl.semaphore_signal(barrier, inc=1, device_id=partner, device_id_type=MESH)

    pair_levels = lax.broadcasted_iota(jnp.int32, (2 * GRID, 128), 0).astype(F32).astype(BF16)
    levels = pair_levels[:GRID]
    row_levels = lax.broadcasted_iota(jnp.int32, (GRID // 2, 128), 0)
    def pair_copy(beam):
        other = pl.ds(pl.multiple_of((1 - core) * 64, 64), 64)
        return remote(grid.at[beam, other], pair_in.at[beam], pair_sem, (beam,), me, member(0, 1))

    def window_copies(beam):
        return [
            remote(
                half.at[beam],
                window_in.at[beam, distance - 1, y_flip],
                window_sem,
                (beam, distance - 1, y_flip),
                behind(-distance if beam == 1 else distance),
                member(y_flip, 0),
            )
            for distance in (2, 3, 1)
            for y_flip in (1, 0)
        ]

    def share_copy(beam):
        rows = pl.ds(pl.multiple_of(core * 64, 64), 64)
        place = spectrum.at[beam, rows]
        return remote(place, place, share_sem, (beam,), me, member(0, 1))

    def leave_copies(beam):
        return [
            remote(
                leavers.at[way, beam],
                arrived.at[beam, :, pl.ds(way * BLOCK, BLOCK)],
                leave_sem,
                (way, beam),
                behind(1 if way == 0 else -1),
                dom,
            )
            for way in range(2)
        ]

    def kick_copies(beam):
        return [
            remote(
                leaver_kicks.at[beam, :, pl.ds((1 - way) * BLOCK, BLOCK)],
                arrived_kicks.at[beam, :, pl.ds(way * BLOCK, BLOCK)],
                kick_sem,
                (way, beam),
                behind(1 if way == 0 else -1),
                dom,
            )
            for way in range(2)
        ]

    def start(copies):
        for copy in copies:
            copy.start()

    def window_send(beam):
        pair_copy(beam).wait_recv()
        mine = pl.ds(pl.multiple_of(core * 64, 64), 64)
        half[beam] = grid[beam, mine, :] + pair_in[beam]
        start(window_copies(beam))

    def share_send(beam):
        for copy in window_copies(beam):
            copy.wait_recv()
        total = window_in[beam, 0, 0]
        for distance in range(SECTIONS):
            for y_flip in (0, 1):
                if distance or y_flip:
                    total = total + window_in[beam, distance, y_flip]
        rows = pl.ds(pl.multiple_of(core * 64, 64), 64)
        spectrum[beam, rows, :] = times_const(total, rights[:, :GRID])
        share_copy(beam).start()

    def solve(beam):
        share_copy(beam).wait_recv()
        scaled = const_times(lefts[:GRID, :], spectrum[beam]) * const[4]
        both = const_times(lefts[GRID:, :], scaled)
        field_x = times_const(both[:GRID], rights[:, :GRID])
        field_y = times_const(both[GRID:], rights[:, GRID:])
        half_grid = GRID // 2
        fields = jnp.concatenate(
            [
                jnp.concatenate([value[:half_grid], value[half_grid:]], axis=1)
                for value in (field_x, field_y)
            ],
            axis=0,
        )
        field[beam] = jnp.concatenate(parts(fields), axis=0)

    row_place = lax.broadcasted_iota(jnp.int32, (BLOCK, 128), 0) * 128 + lax.broadcasted_iota(
        jnp.int32, (BLOCK, 128), 1
    )
    def leave_pack(beam):
        loads["coords", beam].wait()
        for way in range(2):
            rows = slice(ROWS - BLOCK, ROWS) if way == 0 else slice(0, BLOCK)
            limit = (up_count if way == 0 else down_count)[beam]
            base = turn([state[beam, comp, rows, :] for comp in range(4)])
            for comp, value in enumerate((*base, state[beam, 4, rows, :])):
                if way == 0:
                    value = reversed_block(value)
                leavers[way, beam, comp] = jnp.where(row_place < limit, value, 0.0)

    def look_up(beam, first, count):
        rows = pl.ds(pl.multiple_of(first, 8), count)
        kick_x, kick_y = lookup(cell[beam, rows, :], field[1 - beam], pair_levels, row_levels)
        kicks[beam, 0, rows, :] = kick_x
        kicks[beam, 1, rows, :] = kick_y
        shape = (count, 128)
        place = (first + lax.broadcasted_iota(jnp.int32, shape, 0)) * 128
        place = place + lax.broadcasted_iota(jnp.int32, shape, 1)
        stays = (place < ROWS * 128 - counts[beam, 0, 0, 0]) & (place >= counts[beam, 0, 0, 1])
        base = turn([state[beam, comp, rows, :] for comp in range(4)])
        for comp, value in enumerate((*kicked(base, kick_x, kick_y), state[beam, 4, rows, :])):
            kept[beam, comp, rows, :] = jnp.where(stays, value, 0.0)

    def kick_send(beam):
        for comp in range(2):
            down = jnp.where(row_place < down_count[beam], kicks[beam, comp, :BLOCK, :], 0.0)
            up = reversed_block(kicks[beam, comp, ROWS - BLOCK :, :])
            leaver_kicks[beam, comp, :BLOCK, :] = down
            leaver_kicks[beam, comp, BLOCK:, :] = jnp.where(row_place < up_count[beam], up, 0.0)
        start(kick_copies(beam))

    loads["cells", 0].wait()
    loads["weights", 0].wait()
    per_beam = ROWS // DEPOSIT_ROWS

    def deposit_step(i, _):
        beam = i // per_beam
        inner = lax.rem(i, per_beam)

        @pl.when(i == per_beam)
        def _():
            pl.semaphore_wait(barrier, len(partners))
            pair_copy(0).start()
            loads["cells", 1].wait()
            loads["weights", 1].wait()

        @pl.when(i == per_beam + per_beam // 2)
        def _():
            window_send(0)

        rows = pl.ds(pl.multiple_of(inner * DEPOSIT_ROWS, DEPOSIT_ROWS), DEPOSIT_ROWS)
        added = deposit(cell[beam, rows, :], state[beam, 4, rows, :], levels)

        @pl.when(inner == 0)
        def _():
            grid[beam] = added

        @pl.when(inner > 0)
        def _():
            grid[beam] = grid[beam] + added

        return 0

    lax.fori_loop(0, 2 * per_beam, deposit_step, 0)
    pair_copy(1).start()
    loads["counts"].wait()
    up_count = [jnp.where(me == slices - 1, 0, counts[beam, 0, 0, 0]) for beam in range(2)]
    down_count = [jnp.where(me == 0, 0, counts[beam, 0, 0, 1]) for beam in range(2)]
    for beam in range(2):
        leave_pack(beam)
    loads["table"].wait()
    for i in range(3):
        lefts[pl.ds(i * GRID, GRID), :] = left_factor(const[i])
    rights[:, :GRID] = right_factor(const[0])
    rights[:, GRID:] = right_factor(const[3])
    window_send(1)
    share_send(0)
    for beam in range(2):
        start(leave_copies(beam))
    steps = ROWS // 2 // LOOK_ROWS

    def look_step(i, _):
        part = i // steps
        inner = lax.rem(i, steps)
        beam = 1 - lax.rem(part, 2)

        @pl.when((inner == 0) & (part < 2))
        def _():
            solve(1 - beam)

        @pl.when(i == steps // 2)
        def _():
            share_send(1)

        @pl.when(i == steps)
        def _():
            kick_send(1)

        @pl.when(i == 2 * steps)
        def _():
            kick_send(0)

        ends = inner * LOOK_ROWS + jnp.where(inner * LOOK_ROWS >= BLOCK, ROWS - 2 * BLOCK, 0)
        middle = BLOCK + inner * LOOK_ROWS
        look_up(beam, jnp.where(part < 2, ends, middle), LOOK_ROWS)
        return 0

    lax.fori_loop(0, 4 * steps, look_step, 0)
    for beam in range(2):
        for copy in (*leave_copies(beam), *kick_copies(beam)):
            copy.wait()
        for copy in (pair_copy(beam), *window_copies(beam), share_copy(beam)):
            copy.wait_send()


def finish(kept_in, arrived, arrived_kicks, kept, arrivals):
    for beam in range(2):
        kept[beam] = kept_in[beam]
        base = [arrived[beam, comp] for comp in range(4)]
        done = kicked(base, arrived_kicks[beam, 0], arrived_kicks[beam, 1])
        for comp, value in enumerate((*done, arrived[beam, 4])):
            arrivals[beam, comp] = value


def local(slices, particles, cells, counts):
    in_hbm = pl.BlockSpec(memory_space=pltpu.HBM)
    dma = pltpu.SemaphoreType.DMA
    in_vmem = pl.BlockSpec(memory_space=pltpu.VMEM)
    shapes = (
        jax.ShapeDtypeStruct((2, 5, ROWS, 128), F32),
        jax.ShapeDtypeStruct((2, 5, 2 * BLOCK, 128), F32),
    )
    results = pl.pallas_call(
        functools.partial(kernel, slices),
        out_shape=(*shapes, jax.ShapeDtypeStruct((2, 2, 2 * BLOCK, 128), F32)),
        in_specs=[
            in_hbm,
            in_hbm,
            in_hbm,
            in_hbm,
        ],
        out_specs=(in_vmem, in_vmem, in_vmem),
        scratch_shapes=[
            pltpu.VMEM((2, 5, ROWS, 128), F32),
            pltpu.VMEM((2, ROWS, 128), jnp.int32),
            pltpu.VMEM((5, GRID, GRID), F32),
            pltpu.VMEM((3 * GRID, 3 * GRID), BF16),
            pltpu.VMEM((3 * GRID, 2 * GRID), BF16),
            pltpu.SMEM((2, 1, 1, 2), jnp.int32),
            pltpu.VMEM((2, GRID, GRID), F32),
            pltpu.VMEM((2, GRID // 2, GRID), F32),
            pltpu.VMEM((2, GRID // 2, GRID), F32),
            pltpu.VMEM((2, SECTIONS, 2, GRID // 2, GRID), F32),
            pltpu.VMEM((2, GRID, GRID), F32),
            pltpu.VMEM((2, 2 * GRID, 2 * GRID), BF16),
            pltpu.VMEM((2, 2, 5, BLOCK, 128), F32),
            pltpu.VMEM((2, 2, ROWS, 128), F32),
            pltpu.VMEM((2, 2, 2 * BLOCK, 128), F32),
            dma((8,)),
            dma((2, 2)),
            dma((2, 2, SECTIONS, 2)),
            dma((2, 2)),
            dma((2, 2, 2)),
            dma((2, 2, 2)),
        ],
        compiler_params=pltpu.CompilerParams(
            collective_id=0, has_side_effects=True, vmem_limit_bytes=40 * 2**20
        ),
        cost_estimate=pl.CostEstimate(
            flops=7 * 10**9, bytes_accessed=2 * 10**6, transcendentals=0
        ),
        name="crossing",
    )(
        pltpu.with_memory_space_constraint(particles.reshape(2, 5, ROWS, 128), pltpu.HBM),
        pltpu.with_memory_space_constraint(cells.reshape(2, ROWS, 128), pltpu.HBM),
        pltpu.with_memory_space_constraint(counts.transpose(0, 2, 3, 1), pltpu.HBM),
        pltpu.with_memory_space_constraint(jnp.asarray(constants()), pltpu.HBM),
    )
    kept, arrivals = pl.pallas_call(
        finish,
        out_shape=shapes,
        in_specs=[in_vmem, in_vmem, in_vmem],
        out_specs=(in_vmem, in_vmem),
        name="finish",
    )(*(pltpu.with_memory_space_constraint(result, pltpu.VMEM) for result in results))
    return kept.reshape(2, 5, 1, ROWS * 128), arrivals.reshape(2, 5, 1, 2 * BLOCK * 128)


def solution(mesh):
    return jax.shard_map(
        functools.partial(local, mesh.shape["cuts"]),
        mesh=mesh,
        in_specs=(
            P(None, None, "cuts", "dom"),
            P(None, "cuts", "dom"),
            P(None, None, "cuts", "dom"),
        ),
        out_specs=(P(None, None, "cuts", "dom"), P(None, None, "cuts", "dom")),
        check_vma=False,
    )
```

```python
import functools
import math

import jax
import jax.numpy as jnp
import numpy as np
from jax import lax
from jax.experimental import pallas as pl
from jax.experimental.pallas import tpu as pltpu
from jax.sharding import PartitionSpec as P

MESH = pl.DeviceIdType.MESH
GRID = 128
SECTIONS = 3
ROWS = 128
BLOCK = 32
DEPOSIT_ROWS = 64
LOOK_ROWS = 32
KICK_SCALE = 0.01
COS_X, SIN_X = (math.cos(2 * math.pi * 0.31), math.sin(2 * math.pi * 0.31))
COS_Y, SIN_Y = (math.cos(2 * math.pi * 0.32), math.sin(2 * math.pi * 0.32))
F32, BF16 = jnp.float32, jnp.bfloat16


def parts(values):
    high = values.astype(BF16)
    return high, (values - high.astype(F32)).astype(BF16)


def left_factor(a):
    high, low = parts(a)
    return jnp.concatenate([high, high, low], axis=1)


def right_factor(b):
    high, low = parts(b)
    return jnp.concatenate([high, low, high], axis=0)


def constants():
    index = np.arange(1, GRID + 1)
    angle = (index[:, None] * index[None, :] % (2 * (GRID + 1))) * (np.pi / (GRID + 1))
    basis = math.sqrt(2.0 / (GRID + 1)) * np.sin(angle)
    padded = np.pad(basis, ((1, 1), (0, 0)))
    slope = (padded[:-2] - padded[2:]) * (0.5 * KICK_SCALE)
    eigen = 2.0 - 2.0 * np.cos(index * (np.pi / (GRID + 1)))
    inverse = 1.0 / (eigen[:, None] + eigen[None, :])
    order = np.concatenate([np.arange(0, GRID, 2), np.arange(1, GRID, 2)])
    return np.stack([basis, slope[order], basis[order], slope.T, inverse]).astype(np.float32)


def times_const(a, right):
    return jnp.dot(left_factor(a), right, preferred_element_type=F32)


def const_times(left, b):
    return jnp.dot(left, right_factor(b), preferred_element_type=F32)


def across(row):
    return jnp.broadcast_to(row, (GRID, 128))


def deposit(cells, weights, levels):
    row = (cells >> 7).astype(F32).astype(BF16)
    column = (cells & 127).astype(F32).astype(BF16)
    high, low = parts(weights)
    zero, one = jnp.zeros((GRID, 128), BF16), jnp.ones((GRID, 128), BF16)
    hit_column, part_high, part_low = [], [], []
    for i in range(cells.shape[0]):
        here = levels == across(row[i : i + 1])
        part_high.append(jnp.where(here, across(high[i : i + 1]), zero))
        part_low.append(jnp.where(here, across(low[i : i + 1]), zero))
        hit_column.append(jnp.where(levels == across(column[i : i + 1]), one, zero))
    left = jnp.concatenate(
        [jnp.concatenate(part_high, axis=1), jnp.concatenate(part_low, axis=1)], axis=0
    )
    right = jnp.concatenate(hit_column, axis=1)
    both = lax.dot_general(left, right, (((1,), (1,)), ((), ())), preferred_element_type=F32)
    return both[:GRID] + both[GRID:]


def lookup(cells, field, levels, row_levels):
    pair = cells >> 8
    place = (cells & 255).astype(F32).astype(BF16)
    zero, one = jnp.zeros((2 * GRID, 128), BF16), jnp.ones((2 * GRID, 128), BF16)
    half = GRID // 2
    value_x, value_y = [], []
    for first in range(0, cells.shape[0], 2):
        hits = [
            jnp.where(levels == jnp.broadcast_to(place[i : i + 1], (2 * GRID, 128)), one, zero)
            for i in (first, first + 1)
        ]
        picked = jnp.dot(field, jnp.concatenate(hits, axis=1), preferred_element_type=F32)
        for i in (0, 1):
            here = row_levels == jnp.broadcast_to(pair[first + i : first + i + 1], (half, 128))
            part = picked[:, 128 * i : 128 * (i + 1)]
            both_x = part[:half] + part[GRID : GRID + half]
            both_y = part[half:GRID] + part[GRID + half :]
            value_x.append(jnp.sum(jnp.where(here, both_x, 0.0), axis=0, keepdims=True))
            value_y.append(jnp.sum(jnp.where(here, both_y, 0.0), axis=0, keepdims=True))
    return jnp.concatenate(value_x, axis=0), jnp.concatenate(value_y, axis=0)


def reversed_block(block):
    lanes = 127 - lax.broadcasted_iota(jnp.int32, (8, 128), 1)
    rows = 7 - lax.broadcasted_iota(jnp.int32, (8, 128), 0)
    pieces = []
    for i in reversed(range(block.shape[0] // 8)):
        piece = jnp.take_along_axis(block[8 * i : 8 * i + 8], lanes, axis=1)
        pieces.append(jnp.take_along_axis(piece, rows, axis=0))
    return jnp.concatenate(pieces, axis=0)


def turn(state):
    pos_x, mom_x, pos_y, mom_y = state
    return (
        COS_X * pos_x + SIN_X * mom_x,
        -SIN_X * pos_x + COS_X * mom_x,
        COS_Y * pos_y + SIN_Y * mom_y,
        -SIN_Y * pos_y + COS_Y * mom_y,
    )


def kicked(base, kick_x, kick_y):
    return (
        base[0] + SIN_X * kick_x,
        base[1] + COS_X * kick_x,
        base[2] + SIN_Y * kick_y,
        base[3] + COS_Y * kick_y,
    )


def kernel(
    slices,
    particles,
    cells,
    counts_in,
    table,
    kept,
    arrived,
    arrived_kicks,
    state,
    cell,
    const,
    lefts,
    rights,
    counts,
    grid,
    pair_in,
    half,
    window_in,
    spectrum,
    field,
    leavers,
    kicks,
    leaver_kicks,
    in_sem,
    pair_sem,
    window_sem,
    share_sem,
    leave_sem,
    kick_sem,
):
    me = lax.axis_index("cuts")
    dom = lax.axis_index("dom")
    y_hi, core = dom // 2, dom % 2

    def behind(distance):
        return lax.rem(me + (distance + slices), slices)

    def member(y_flip, core_flip):
        y = 1 - y_hi if y_flip else y_hi
        c = 1 - core if core_flip else core
        return y * 2 + c

    def remote(src, dst, sems, index, cut, member_no):
        copy = pltpu.make_async_remote_copy(
            src_ref=src,
            dst_ref=dst,
            send_sem=sems.at[(0, *index)],
            recv_sem=sems.at[(1, *index)],
            device_id=(cut, member_no),
            device_id_type=MESH,
        )
        return copy

    ring = slices // 2
    place_in_ring = lax.rem(me, ring)
    lead = jnp.where(place_in_ring < ring // 2, 1, 0)
    use_first = lead
    loads = {}
    for turn_no in range(2):
        beam = lead if turn_no == 0 else 1 - lead
        loads["cells", turn_no] = pltpu.make_async_copy(
            cells.at[beam], cell.at[beam], in_sem.at[turn_no]
        )
        loads["weights", turn_no] = pltpu.make_async_copy(
            particles.at[beam, 4], state.at[beam, 4], in_sem.at[2 + turn_no]
        )
    for beam in (0, 1):
        loads["coords", beam] = pltpu.make_async_copy(
            particles.at[beam, pl.ds(0, 4)], state.at[beam, pl.ds(0, 4)], in_sem.at[4 + beam]
        )
    loads["table"] = pltpu.make_async_copy(table, const, in_sem.at[6])
    loads["counts"] = pltpu.make_async_copy(counts_in, counts, in_sem.at[7])
    for load in loads.values():
        load.start()

    barrier = pltpu.get_barrier_semaphore()
    partners = [(me, member(0, 1))]
    for distance in range(1, SECTIONS + 1):
        for sign in (1, -1):
            for y_flip in (0, 1):
                partners.append((behind(sign * distance), member(y_flip, 0)))
    for partner in partners:
        pl.semaphore_signal(barrier, inc=1, device_id=partner, device_id_type=MESH)

    pair_levels = lax.broadcasted_iota(jnp.int32, (2 * GRID, 128), 0).astype(F32).astype(BF16)
    levels = pair_levels[:GRID]
    row_levels = lax.broadcasted_iota(jnp.int32, (GRID // 2, 128), 0)
    def pair_copy(beam):
        other = pl.ds(pl.multiple_of((1 - core) * 64, 64), 64)
        return remote(grid.at[beam, other], pair_in.at[beam], pair_sem, (beam,), me, member(0, 1))

    def window_copies(beam):
        return [
            remote(
                half.at[beam],
                window_in.at[beam, distance - 1, y_flip],
                window_sem,
                (beam, distance - 1, y_flip),
                behind(distance * (1 - 2 * beam)),
                member(y_flip, 0),
            )
            for distance in (2, 3, 1)
            for y_flip in (1, 0)
        ]

    def share_copy(beam):
        rows = pl.ds(pl.multiple_of(core * 64, 64), 64)
        place = spectrum.at[beam, rows]
        return remote(place, place, share_sem, (beam,), me, member(0, 1))

    def leave_copies(beam):
        return [
            remote(
                leavers.at[way, beam],
                arrived.at[beam, :, pl.ds(way * BLOCK, BLOCK)],
                leave_sem,
                (way, beam),
                behind(1 if way == 0 else -1),
                dom,
            )
            for way in range(2)
        ]

    def kick_copies(beam):
        return [
            remote(
                leaver_kicks.at[beam, :, pl.ds((1 - way) * BLOCK, BLOCK)],
                arrived_kicks.at[beam, :, pl.ds(way * BLOCK, BLOCK)],
                kick_sem,
                (way, beam),
                behind(1 if way == 0 else -1),
                dom,
            )
            for way in range(2)
        ]

    def start(copies):
        for copy in copies:
            copy.start()

    def window_send(beam):
        pair_copy(beam).wait_recv()
        mine = pl.ds(pl.multiple_of(core * 64, 64), 64)
        half[beam] = grid[beam, mine, :] + pair_in[beam]
        start(window_copies(beam))

    def share_send(beam):
        for copy in window_copies(beam):
            copy.wait_recv()
        total = window_in[beam, 0, 0]
        for distance in range(SECTIONS):
            for y_flip in (0, 1):
                if distance or y_flip:
                    total = total + window_in[beam, distance, y_flip]
        rows = pl.ds(pl.multiple_of(core * 64, 64), 64)
        spectrum[beam, rows, :] = times_const(total, rights[:, :GRID])
        share_copy(beam).start()

    def solve(beam):
        share_copy(beam).wait_recv()
        scaled = const_times(lefts[:GRID, :], spectrum[beam]) * const[4]
        both = const_times(lefts[GRID:, :], scaled)
        field_x = times_const(both[:GRID], rights[:, :GRID])
        field_y = times_const(both[GRID:], rights[:, GRID:])
        half_grid = GRID // 2
        fields = jnp.concatenate(
            [
                jnp.concatenate([value[:half_grid], value[half_grid:]], axis=1)
                for value in (field_x, field_y)
            ],
            axis=0,
        )
        field[beam] = jnp.concatenate(parts(fields), axis=0)

    row_place = lax.broadcasted_iota(jnp.int32, (BLOCK, 128), 0) * 128 + lax.broadcasted_iota(
        jnp.int32, (BLOCK, 128), 1
    )
    def leaver_counts(beam):
        up = jnp.where(me == slices - 1, 0, counts[beam, 0, 0, 0])
        return up, jnp.where(me == 0, 0, counts[beam, 0, 0, 1])

    def leave_pack(beam):
        loads["coords", beam].wait()
        for way in range(2):
            rows = slice(ROWS - BLOCK, ROWS) if way == 0 else slice(0, BLOCK)
            limit = leaver_counts(beam)[way]
            base = turn([state[beam, comp, rows, :] for comp in range(4)])
            for comp, value in enumerate((*base, state[beam, 4, rows, :])):
                if way == 0:
                    value = reversed_block(value)
                leavers[way, beam, comp] = jnp.where(row_place < limit, value, 0.0)

    def look_up(beam, first, count):
        rows = pl.ds(pl.multiple_of(first, 8), count)
        kick_x, kick_y = lookup(cell[beam, rows, :], field[1 - beam], pair_levels, row_levels)
        kicks[beam, 0, rows, :] = kick_x
        kicks[beam, 1, rows, :] = kick_y
        shape = (count, 128)
        place = (first + lax.broadcasted_iota(jnp.int32, shape, 0)) * 128
        place = place + lax.broadcasted_iota(jnp.int32, shape, 1)
        stays = (place < ROWS * 128 - counts[beam, 0, 0, 0]) & (place >= counts[beam, 0, 0, 1])
        base = turn([state[beam, comp, rows, :] for comp in range(4)])
        for comp, value in enumerate((*kicked(base, kick_x, kick_y), state[beam, 4, rows, :])):
            kept[beam, comp, rows, :] = jnp.where(stays, value, 0.0)

    def kick_send(beam):
        up_count, down_count = leaver_counts(beam)
        for comp in range(2):
            down = jnp.where(row_place < down_count, kicks[beam, comp, :BLOCK, :], 0.0)
            up = reversed_block(kicks[beam, comp, ROWS - BLOCK :, :])
            leaver_kicks[beam, comp, :BLOCK, :] = down
            leaver_kicks[beam, comp, BLOCK:, :] = jnp.where(row_place < up_count, up, 0.0)
        start(kick_copies(beam))

    loads["cells", 0].wait()
    loads["weights", 0].wait()
    per_beam = ROWS // DEPOSIT_ROWS

    def deposit_step(i, _):
        beam = jnp.where(i < per_beam, lead, 1 - lead)
        inner = lax.rem(i, per_beam)

        @pl.when(i == per_beam)
        def _():
            pl.semaphore_wait(barrier, len(partners))
            pair_copy(lead).start()
            loads["cells", 1].wait()
            loads["weights", 1].wait()

        @pl.when(i == per_beam + per_beam // 2)
        def _():
            window_send(lead)

        rows = pl.ds(pl.multiple_of(inner * DEPOSIT_ROWS, DEPOSIT_ROWS), DEPOSIT_ROWS)
        added = deposit(cell[beam, rows, :], state[beam, 4, rows, :], levels)

        @pl.when(inner == 0)
        def _():
            grid[beam] = added

        @pl.when(inner > 0)
        def _():
            grid[beam] = grid[beam] + added

        return 0

    lax.fori_loop(0, 2 * per_beam, deposit_step, 0)
    pair_copy(1 - lead).start()
    loads["table"].wait()
    for i in range(3):
        lefts[pl.ds(i * GRID, GRID), :] = left_factor(const[i])
    rights[:, :GRID] = right_factor(const[0])
    rights[:, GRID:] = right_factor(const[3])
    window_send(1 - lead)
    loads["counts"].wait()
    for beam in range(2):
        leave_pack(beam)
    share_send(use_first)
    for beam in range(2):
        start(leave_copies(beam))
    steps = ROWS // 2 // LOOK_ROWS

    def look_step(i, _):
        part = i // steps
        inner = lax.rem(i, steps)
        beam = jnp.where(lax.rem(part, 2) == 0, 1 - use_first, use_first)

        @pl.when((inner == 0) & (part < 2))
        def _():
            solve(1 - beam)

        @pl.when(i == steps // 2)
        def _():
            share_send(1 - use_first)

        @pl.when(i == steps)
        def _():
            kick_send(1 - use_first)

        @pl.when(i == 2 * steps)
        def _():
            kick_send(use_first)

        ends = inner * LOOK_ROWS + jnp.where(inner * LOOK_ROWS >= BLOCK, ROWS - 2 * BLOCK, 0)
        middle = BLOCK + inner * LOOK_ROWS
        look_up(beam, jnp.where(part < 2, ends, middle), LOOK_ROWS)
        return 0

    lax.fori_loop(0, 4 * steps, look_step, 0)
    for beam in range(2):
        for copy in (*leave_copies(beam), *kick_copies(beam)):
            copy.wait()
        for copy in (pair_copy(beam), *window_copies(beam), share_copy(beam)):
            copy.wait_send()


def finish(kept_in, arrived, arrived_kicks, kept, arrivals):
    for beam in range(2):
        kept[beam] = kept_in[beam]
        base = [arrived[beam, comp] for comp in range(4)]
        done = kicked(base, arrived_kicks[beam, 0], arrived_kicks[beam, 1])
        for comp, value in enumerate((*done, arrived[beam, 4])):
            arrivals[beam, comp] = value


def local(slices, particles, cells, counts):
    in_hbm = pl.BlockSpec(memory_space=pltpu.HBM)
    dma = pltpu.SemaphoreType.DMA
    in_vmem = pl.BlockSpec(memory_space=pltpu.VMEM)
    shapes = (
        jax.ShapeDtypeStruct((2, 5, ROWS, 128), F32),
        jax.ShapeDtypeStruct((2, 5, 2 * BLOCK, 128), F32),
    )
    results = pl.pallas_call(
        functools.partial(kernel, slices),
        out_shape=(*shapes, jax.ShapeDtypeStruct((2, 2, 2 * BLOCK, 128), F32)),
        in_specs=[
            in_hbm,
            in_hbm,
            in_hbm,
            in_hbm,
        ],
        out_specs=(in_vmem, in_vmem, in_vmem),
        scratch_shapes=[
            pltpu.VMEM((2, 5, ROWS, 128), F32),
            pltpu.VMEM((2, ROWS, 128), jnp.int32),
            pltpu.VMEM((5, GRID, GRID), F32),
            pltpu.VMEM((3 * GRID, 3 * GRID), BF16),
            pltpu.VMEM((3 * GRID, 2 * GRID), BF16),
            pltpu.SMEM((2, 1, 1, 2), jnp.int32),
            pltpu.VMEM((2, GRID, GRID), F32),
            pltpu.VMEM((2, GRID // 2, GRID), F32),
            pltpu.VMEM((2, GRID // 2, GRID), F32),
            pltpu.VMEM((2, SECTIONS, 2, GRID // 2, GRID), F32),
            pltpu.VMEM((2, GRID, GRID), F32),
            pltpu.VMEM((2, 2 * GRID, 2 * GRID), BF16),
            pltpu.VMEM((2, 2, 5, BLOCK, 128), F32),
            pltpu.VMEM((2, 2, ROWS, 128), F32),
            pltpu.VMEM((2, 2, 2 * BLOCK, 128), F32),
            dma((8,)),
            dma((2, 2)),
            dma((2, 2, SECTIONS, 2)),
            dma((2, 2)),
            dma((2, 2, 2)),
            dma((2, 2, 2)),
        ],
        compiler_params=pltpu.CompilerParams(
            collective_id=0, has_side_effects=True, vmem_limit_bytes=40 * 2**20
        ),
        cost_estimate=pl.CostEstimate(
            flops=7 * 10**9, bytes_accessed=2 * 10**6, transcendentals=0
        ),
        name="crossing",
    )(
        pltpu.with_memory_space_constraint(particles.reshape(2, 5, ROWS, 128), pltpu.HBM),
        pltpu.with_memory_space_constraint(cells.reshape(2, ROWS, 128), pltpu.HBM),
        pltpu.with_memory_space_constraint(counts.transpose(0, 2, 3, 1), pltpu.HBM),
        pltpu.with_memory_space_constraint(jnp.asarray(constants()), pltpu.HBM),
    )
    kept, arrivals = pl.pallas_call(
        finish,
        out_shape=shapes,
        in_specs=[in_vmem, in_vmem, in_vmem],
        out_specs=(in_vmem, in_vmem),
        name="finish",
    )(*(pltpu.with_memory_space_constraint(result, pltpu.VMEM) for result in results))
    return kept.reshape(2, 5, 1, ROWS * 128), arrivals.reshape(2, 5, 1, 2 * BLOCK * 128)


def solution(mesh):
    return jax.shard_map(
        functools.partial(local, mesh.shape["cuts"]),
        mesh=mesh,
        in_specs=(
            P(None, None, "cuts", "dom"),
            P(None, "cuts", "dom"),
            P(None, None, "cuts", "dom"),
        ),
        out_specs=(P(None, None, "cuts", "dom"), P(None, None, "cuts", "dom")),
        check_vma=False,
    )
```

```python
import functools
import math

import jax
import jax.numpy as jnp
import numpy as np
from jax import lax
from jax.experimental import pallas as pl
from jax.experimental.pallas import tpu as pltpu
from jax.sharding import PartitionSpec as P

MESH = pl.DeviceIdType.MESH
GRID = 128
SECTIONS = 3
ROWS = 128
BLOCK = 32
DEPOSIT_ROWS = 64
KICK_SCALE = 0.01
COS_X, SIN_X = (math.cos(2 * math.pi * 0.31), math.sin(2 * math.pi * 0.31))
COS_Y, SIN_Y = (math.cos(2 * math.pi * 0.32), math.sin(2 * math.pi * 0.32))
F32, BF16 = jnp.float32, jnp.bfloat16


def parts(values):
    high = values.astype(BF16)
    return high, (values - high.astype(F32)).astype(BF16)


def left_factor(a):
    high, low = parts(a)
    return jnp.concatenate([high, high, low], axis=1)


def right_factor(b):
    high, low = parts(b)
    return jnp.concatenate([high, low, high], axis=0)


def constants():
    index = np.arange(1, GRID + 1)
    angle = (index[:, None] * index[None, :] % (2 * (GRID + 1))) * (np.pi / (GRID + 1))
    basis = math.sqrt(2.0 / (GRID + 1)) * np.sin(angle)
    padded = np.pad(basis, ((1, 1), (0, 0)))
    slope = (padded[:-2] - padded[2:]) * (0.5 * KICK_SCALE)
    eigen = 2.0 - 2.0 * np.cos(index * (np.pi / (GRID + 1)))
    inverse = 1.0 / (eigen[:, None] + eigen[None, :])
    order = np.concatenate([np.arange(0, GRID, 2), np.arange(1, GRID, 2)])
    return np.stack([basis, slope[order], basis[order], slope.T, inverse]).astype(np.float32)


def times_const(a, right):
    return jnp.dot(left_factor(a), right, preferred_element_type=F32)


def const_times(left, b):
    return jnp.dot(left, right_factor(b), preferred_element_type=F32)


def across(row):
    return jnp.broadcast_to(row, (GRID, 128))


def deposit(cells, weights, levels):
    row = (cells >> 7).astype(F32).astype(BF16)
    column = (cells & 127).astype(F32).astype(BF16)
    high, low = parts(weights)
    zero, one = jnp.zeros((GRID, 128), BF16), jnp.ones((GRID, 128), BF16)
    hit_column, part_high, part_low = [], [], []
    for i in range(cells.shape[0]):
        here = levels == across(row[i : i + 1])
        part_high.append(jnp.where(here, across(high[i : i + 1]), zero))
        part_low.append(jnp.where(here, across(low[i : i + 1]), zero))
        hit_column.append(jnp.where(levels == across(column[i : i + 1]), one, zero))
    left = jnp.concatenate(
        [jnp.concatenate(part_high, axis=1), jnp.concatenate(part_low, axis=1)], axis=0
    )
    right = jnp.concatenate(hit_column, axis=1)
    both = lax.dot_general(left, right, (((1,), (1,)), ((), ())), preferred_element_type=F32)
    return both[:GRID] + both[GRID:]


def lookup(cells, field, levels, row_levels):
    pair = cells >> 8
    place = (cells & 255).astype(F32).astype(BF16)
    zero, one = jnp.zeros((2 * GRID, 128), BF16), jnp.ones((2 * GRID, 128), BF16)
    half = GRID // 2
    value_x, value_y = [], []
    for first in range(0, cells.shape[0], 2):
        hits = [
            jnp.where(levels == jnp.broadcast_to(place[i : i + 1], (2 * GRID, 128)), one, zero)
            for i in (first, first + 1)
        ]
        picked = jnp.dot(field, jnp.concatenate(hits, axis=1), preferred_element_type=F32)
        for i in (0, 1):
            here = row_levels == jnp.broadcast_to(pair[first + i : first + i + 1], (half, 128))
            part = picked[:, 128 * i : 128 * (i + 1)]
            both_x = part[:half] + part[GRID : GRID + half]
            both_y = part[half:GRID] + part[GRID + half :]
            value_x.append(jnp.sum(jnp.where(here, both_x, 0.0), axis=0, keepdims=True))
            value_y.append(jnp.sum(jnp.where(here, both_y, 0.0), axis=0, keepdims=True))
    return jnp.concatenate(value_x, axis=0), jnp.concatenate(value_y, axis=0)


def reversed_block(block):
    lanes = 127 - lax.broadcasted_iota(jnp.int32, (8, 128), 1)
    rows = 7 - lax.broadcasted_iota(jnp.int32, (8, 128), 0)
    pieces = []
    for i in reversed(range(block.shape[0] // 8)):
        piece = jnp.take_along_axis(block[8 * i : 8 * i + 8], lanes, axis=1)
        pieces.append(jnp.take_along_axis(piece, rows, axis=0))
    return jnp.concatenate(pieces, axis=0)


def turn(state):
    pos_x, mom_x, pos_y, mom_y = state
    return (
        COS_X * pos_x + SIN_X * mom_x,
        -SIN_X * pos_x + COS_X * mom_x,
        COS_Y * pos_y + SIN_Y * mom_y,
        -SIN_Y * pos_y + COS_Y * mom_y,
    )


def kicked(base, kick_x, kick_y):
    return (
        base[0] + SIN_X * kick_x,
        base[1] + COS_X * kick_x,
        base[2] + SIN_Y * kick_y,
        base[3] + COS_Y * kick_y,
    )


def kernel(
    slices,
    particles,
    cells,
    counts_in,
    table,
    kept,
    arrived,
    arrived_kicks,
    state,
    cell,
    const,
    lefts,
    rights,
    counts,
    grid,
    pair_in,
    half,
    window_in,
    spectrum,
    field,
    leavers,
    kicks,
    leaver_kicks,
    in_sem,
    pair_sem,
    window_sem,
    share_sem,
    leave_sem,
    kick_sem,
):
    me = lax.axis_index("cuts")
    dom = lax.axis_index("dom")
    y_hi, core = dom // 2, dom % 2

    def behind(distance):
        return lax.rem(me + (distance + slices), slices)

    def member(y_flip, core_flip):
        y = 1 - y_hi if y_flip else y_hi
        c = 1 - core if core_flip else core
        return y * 2 + c

    def remote(src, dst, sems, index, cut, member_no):
        copy = pltpu.make_async_remote_copy(
            src_ref=src,
            dst_ref=dst,
            send_sem=sems.at[(0, *index)],
            recv_sem=sems.at[(1, *index)],
            device_id=(cut, member_no),
            device_id_type=MESH,
        )
        return copy

    ring = slices // 2
    place_in_ring = lax.rem(me, ring)
    lead = jnp.where(place_in_ring < ring // 2, 1, 0)
    use_first = lead
    second = jnp.where(place_in_ring >= ring // 2, 2, 3)
    loads = {}
    for turn_no in range(2):
        beam = lead if turn_no == 0 else 1 - lead
        loads["cells", turn_no] = pltpu.make_async_copy(
            cells.at[beam], cell.at[beam], in_sem.at[turn_no]
        )
        loads["weights", turn_no] = pltpu.make_async_copy(
            particles.at[beam, 4], state.at[beam, 4], in_sem.at[2 + turn_no]
        )
    for beam in (0, 1):
        loads["coords", beam] = pltpu.make_async_copy(
            particles.at[beam, pl.ds(0, 4)], state.at[beam, pl.ds(0, 4)], in_sem.at[4 + beam]
        )
    loads["table"] = pltpu.make_async_copy(table, const, in_sem.at[6])
    loads["counts"] = pltpu.make_async_copy(counts_in, counts, in_sem.at[7])
    for load in loads.values():
        load.start()

    barrier = pltpu.get_barrier_semaphore()
    partners = [(me, member(0, 1))]
    for distance in range(1, SECTIONS + 1):
        for sign in (1, -1):
            for y_flip in (0, 1):
                partners.append((behind(sign * distance), member(y_flip, 0)))
    for partner in partners:
        pl.semaphore_signal(barrier, inc=1, device_id=partner, device_id_type=MESH)

    pair_levels = lax.broadcasted_iota(jnp.int32, (2 * GRID, 128), 0).astype(F32).astype(BF16)
    levels = pair_levels[:GRID]
    row_levels = lax.broadcasted_iota(jnp.int32, (GRID // 2, 128), 0)
    def pair_copy(beam):
        other = pl.ds(pl.multiple_of((1 - core) * 64, 64), 64)
        return remote(grid.at[beam, other], pair_in.at[beam], pair_sem, (beam,), me, member(0, 1))

    def window_copies(beam):
        return [
            remote(
                half.at[beam],
                window_in.at[beam, distance - 1, y_flip],
                window_sem,
                (beam, distance - 1, y_flip),
                behind(distance * (1 - 2 * beam)),
                member(y_flip, 0),
            )
            for distance in (2, 3, 1)
            for y_flip in (1, 0)
        ]

    def share_copy(beam):
        rows = pl.ds(pl.multiple_of(core * 64, 64), 64)
        place = spectrum.at[beam, rows]
        return remote(place, place, share_sem, (beam,), me, member(0, 1))

    def leave_copies(beam):
        return [
            remote(
                leavers.at[way, beam],
                arrived.at[beam, :, pl.ds(way * BLOCK, BLOCK)],
                leave_sem,
                (way, beam),
                behind(1 if way == 0 else -1),
                dom,
            )
            for way in range(2)
        ]

    def kick_copy(beam, way):
        return remote(
            leaver_kicks.at[beam, :, pl.ds((1 - way) * BLOCK, BLOCK)],
            arrived_kicks.at[beam, :, pl.ds(way * BLOCK, BLOCK)],
            kick_sem,
            (way, beam),
            behind(1 if way == 0 else -1),
            dom,
        )

    def start(copies):
        for copy in copies:
            copy.start()

    def window_send(beam):
        pair_copy(beam).wait_recv()
        mine = pl.ds(pl.multiple_of(core * 64, 64), 64)
        half[beam] = grid[beam, mine, :] + pair_in[beam]
        start(window_copies(beam))

    def share_send(beam):
        for copy in window_copies(beam):
            copy.wait_recv()
        total = window_in[beam, 0, 0]
        for distance in range(SECTIONS):
            for y_flip in (0, 1):
                if distance or y_flip:
                    total = total + window_in[beam, distance, y_flip]
        rows = pl.ds(pl.multiple_of(core * 64, 64), 64)
        spectrum[beam, rows, :] = times_const(total, rights[:, :GRID])
        share_copy(beam).start()

    def solve(beam):
        share_copy(beam).wait_recv()
        scaled = const_times(lefts[:GRID, :], spectrum[beam]) * const[4]
        both = const_times(lefts[GRID:, :], scaled)
        field_x = times_const(both[:GRID], rights[:, :GRID])
        field_y = times_const(both[GRID:], rights[:, GRID:])
        half_grid = GRID // 2
        fields = jnp.concatenate(
            [
                jnp.concatenate([value[:half_grid], value[half_grid:]], axis=1)
                for value in (field_x, field_y)
            ],
            axis=0,
        )
        field[beam] = jnp.concatenate(parts(fields), axis=0)

    row_place = lax.broadcasted_iota(jnp.int32, (BLOCK, 128), 0) * 128 + lax.broadcasted_iota(
        jnp.int32, (BLOCK, 128), 1
    )
    def leaver_counts(beam):
        up = jnp.where(me == slices - 1, 0, counts[beam, 0, 0, 0])
        return up, jnp.where(me == 0, 0, counts[beam, 0, 0, 1])

    def leave_pack(beam):
        loads["coords", beam].wait()
        for way in range(2):
            rows = slice(ROWS - BLOCK, ROWS) if way == 0 else slice(0, BLOCK)
            limit = leaver_counts(beam)[way]
            base = turn([state[beam, comp, rows, :] for comp in range(4)])
            for comp, value in enumerate((*base, state[beam, 4, rows, :])):
                if way == 0:
                    value = reversed_block(value)
                leavers[way, beam, comp] = jnp.where(row_place < limit, value, 0.0)

    def look_up(beam, first, count):
        rows = pl.ds(pl.multiple_of(first, 8), count)
        kick_x, kick_y = lookup(cell[beam, rows, :], field[1 - beam], pair_levels, row_levels)
        kicks[beam, 0, rows, :] = kick_x
        kicks[beam, 1, rows, :] = kick_y
        shape = (count, 128)
        place = (first + lax.broadcasted_iota(jnp.int32, shape, 0)) * 128
        place = place + lax.broadcasted_iota(jnp.int32, shape, 1)
        stays = (place < ROWS * 128 - counts[beam, 0, 0, 0]) & (place >= counts[beam, 0, 0, 1])
        base = turn([state[beam, comp, rows, :] for comp in range(4)])
        for comp, value in enumerate((*kicked(base, kick_x, kick_y), state[beam, 4, rows, :])):
            kept[beam, comp, rows, :] = jnp.where(stays, value, 0.0)

    def kick_send(beam, way):
        limit = leaver_counts(beam)[way]
        rows = slice(ROWS - BLOCK, ROWS) if way == 0 else slice(0, BLOCK)
        place = slice((1 - way) * BLOCK, (2 - way) * BLOCK)
        for comp in range(2):
            kick = kicks[beam, comp, rows, :]
            if way == 0:
                kick = reversed_block(kick)
            leaver_kicks[beam, comp, place, :] = jnp.where(row_place < limit, kick, 0.0)
        kick_copy(beam, way).start()

    loads["cells", 0].wait()
    loads["weights", 0].wait()
    per_beam = ROWS // DEPOSIT_ROWS

    def deposit_step(i, _):
        beam = jnp.where(i < per_beam, lead, 1 - lead)
        inner = lax.rem(i, per_beam)

        @pl.when(i == per_beam)
        def _():
            pl.semaphore_wait(barrier, len(partners))
            pair_copy(lead).start()
            loads["cells", 1].wait()
            loads["weights", 1].wait()

        @pl.when(i == per_beam + per_beam // 2)
        def _():
            window_send(lead)

        rows = pl.ds(pl.multiple_of(inner * DEPOSIT_ROWS, DEPOSIT_ROWS), DEPOSIT_ROWS)
        added = deposit(cell[beam, rows, :], state[beam, 4, rows, :], levels)

        @pl.when(inner == 0)
        def _():
            grid[beam] = added

        @pl.when(inner > 0)
        def _():
            grid[beam] = grid[beam] + added

        return 0

    lax.fori_loop(0, 2 * per_beam, deposit_step, 0)
    pair_copy(1 - lead).start()
    loads["table"].wait()
    for i in range(3):
        lefts[pl.ds(i * GRID, GRID), :] = left_factor(const[i])
    rights[:, :GRID] = right_factor(const[0])
    rights[:, GRID:] = right_factor(const[3])
    window_send(1 - lead)
    loads["counts"].wait()
    for beam in range(2):
        leave_pack(beam)
    share_send(use_first)
    for beam in range(2):
        start(leave_copies(beam))

    def look_step(i, _):
        now = jnp.where((i == second) | (i == second + 1) | (i > 5), use_first, 1 - use_first)
        block = jnp.where((i == 5) | (i == 7), 2, 1)
        block = jnp.where((i == 1) | (i == second + 1), 0, block)
        block = jnp.where((i == 0) | (i == second), 3, block)
        before = jnp.where(i > second, use_first, 1 - use_first)

        @pl.when((i == 0) | (i == second))
        def _():
            solve(1 - now)

        @pl.when(i == second - 1)
        def _():
            share_send(1 - use_first)

        @pl.when((i == 1) | (i == second + 1))
        def _():
            kick_send(before, 0)

        @pl.when((i == 2) | (i == second + 2))
        def _():
            kick_send(before, 1)

        look_up(now, block * BLOCK, BLOCK)
        return 0

    lax.fori_loop(0, 8, look_step, 0)
    for beam in range(2):
        for copy in (*leave_copies(beam), kick_copy(beam, 0), kick_copy(beam, 1)):
            copy.wait()
        for copy in (pair_copy(beam), *window_copies(beam), share_copy(beam)):
            copy.wait_send()


def finish(kept_in, arrived, arrived_kicks, kept, arrivals):
    for beam in range(2):
        kept[beam] = kept_in[beam]
        base = [arrived[beam, comp] for comp in range(4)]
        done = kicked(base, arrived_kicks[beam, 0], arrived_kicks[beam, 1])
        for comp, value in enumerate((*done, arrived[beam, 4])):
            arrivals[beam, comp] = value


def local(slices, particles, cells, counts):
    in_hbm = pl.BlockSpec(memory_space=pltpu.HBM)
    dma = pltpu.SemaphoreType.DMA
    in_vmem = pl.BlockSpec(memory_space=pltpu.VMEM)
    shapes = (
        jax.ShapeDtypeStruct((2, 5, ROWS, 128), F32),
        jax.ShapeDtypeStruct((2, 5, 2 * BLOCK, 128), F32),
    )
    results = pl.pallas_call(
        functools.partial(kernel, slices),
        out_shape=(*shapes, jax.ShapeDtypeStruct((2, 2, 2 * BLOCK, 128), F32)),
        in_specs=[
            in_hbm,
            in_hbm,
            in_hbm,
            in_hbm,
        ],
        out_specs=(in_vmem, in_vmem, in_vmem),
        scratch_shapes=[
            pltpu.VMEM((2, 5, ROWS, 128), F32),
            pltpu.VMEM((2, ROWS, 128), jnp.int32),
            pltpu.VMEM((5, GRID, GRID), F32),
            pltpu.VMEM((3 * GRID, 3 * GRID), BF16),
            pltpu.VMEM((3 * GRID, 2 * GRID), BF16),
            pltpu.SMEM((2, 1, 1, 2), jnp.int32),
            pltpu.VMEM((2, GRID, GRID), F32),
            pltpu.VMEM((2, GRID // 2, GRID), F32),
            pltpu.VMEM((2, GRID // 2, GRID), F32),
            pltpu.VMEM((2, SECTIONS, 2, GRID // 2, GRID), F32),
            pltpu.VMEM((2, GRID, GRID), F32),
            pltpu.VMEM((2, 2 * GRID, 2 * GRID), BF16),
            pltpu.VMEM((2, 2, 5, BLOCK, 128), F32),
            pltpu.VMEM((2, 2, ROWS, 128), F32),
            pltpu.VMEM((2, 2, 2 * BLOCK, 128), F32),
            dma((8,)),
            dma((2, 2)),
            dma((2, 2, SECTIONS, 2)),
            dma((2, 2)),
            dma((2, 2, 2)),
            dma((2, 2, 2)),
        ],
        compiler_params=pltpu.CompilerParams(
            collective_id=0, has_side_effects=True, vmem_limit_bytes=40 * 2**20
        ),
        cost_estimate=pl.CostEstimate(
            flops=7 * 10**9, bytes_accessed=2 * 10**6, transcendentals=0
        ),
        name="crossing",
    )(
        pltpu.with_memory_space_constraint(particles.reshape(2, 5, ROWS, 128), pltpu.HBM),
        pltpu.with_memory_space_constraint(cells.reshape(2, ROWS, 128), pltpu.HBM),
        pltpu.with_memory_space_constraint(counts.transpose(0, 2, 3, 1), pltpu.HBM),
        pltpu.with_memory_space_constraint(jnp.asarray(constants()), pltpu.HBM),
    )
    kept, arrivals = pl.pallas_call(
        finish,
        out_shape=shapes,
        in_specs=[in_vmem, in_vmem, in_vmem],
        out_specs=(in_vmem, in_vmem),
        name="finish",
    )(*(pltpu.with_memory_space_constraint(result, pltpu.VMEM) for result in results))
    return kept.reshape(2, 5, 1, ROWS * 128), arrivals.reshape(2, 5, 1, 2 * BLOCK * 128)


def solution(mesh):
    return jax.shard_map(
        functools.partial(local, mesh.shape["cuts"]),
        mesh=mesh,
        in_specs=(
            P(None, None, "cuts", "dom"),
            P(None, "cuts", "dom"),
            P(None, None, "cuts", "dom"),
        ),
        out_specs=(P(None, None, "cuts", "dom"), P(None, None, "cuts", "dom")),
        check_vma=False,
    )
```

```python
import functools
import math

import jax
import jax.numpy as jnp
import numpy as np
from jax import lax
from jax.experimental import pallas as pl
from jax.experimental.pallas import tpu as pltpu
from jax.sharding import PartitionSpec as P

MESH = pl.DeviceIdType.MESH
GRID = 128
SECTIONS = 3
ROWS = 128
BLOCK = 32
DEPOSIT_ROWS = 64
KICK_SCALE = 0.01
COS_X, SIN_X = (math.cos(2 * math.pi * 0.31), math.sin(2 * math.pi * 0.31))
COS_Y, SIN_Y = (math.cos(2 * math.pi * 0.32), math.sin(2 * math.pi * 0.32))
F32, BF16 = jnp.float32, jnp.bfloat16


def parts(values):
    high = values.astype(BF16)
    return high, (values - high.astype(F32)).astype(BF16)


def left_factor(a):
    high, low = parts(a)
    return jnp.concatenate([high, high, low], axis=1)


def right_factor(b):
    high, low = parts(b)
    return jnp.concatenate([high, low, high], axis=0)


def constants():
    index = np.arange(1, GRID + 1)
    angle = (index[:, None] * index[None, :] % (2 * (GRID + 1))) * (np.pi / (GRID + 1))
    basis = math.sqrt(2.0 / (GRID + 1)) * np.sin(angle)
    padded = np.pad(basis, ((1, 1), (0, 0)))
    slope = (padded[:-2] - padded[2:]) * (0.5 * KICK_SCALE)
    eigen = 2.0 - 2.0 * np.cos(index * (np.pi / (GRID + 1)))
    inverse = 1.0 / (eigen[:, None] + eigen[None, :])
    order = np.concatenate([np.arange(0, GRID, 2), np.arange(1, GRID, 2)])
    return np.stack([basis, slope[order], basis[order], slope.T, inverse]).astype(np.float32)


def times_const(a, right):
    return jnp.dot(left_factor(a), right, preferred_element_type=F32)


def const_times(left, b):
    return jnp.dot(left, right_factor(b), preferred_element_type=F32)


def across(row):
    return jnp.broadcast_to(row, (GRID, 128))


def deposit(cells, weights, first_row, levels):
    half_grid = GRID // 2
    row = ((cells >> 7) - first_row).astype(F32).astype(BF16)
    column = (cells & 127).astype(F32).astype(BF16)
    high, low = parts(weights)
    zero, one = jnp.zeros((GRID, 128), BF16), jnp.ones((GRID, 128), BF16)
    hit_column, part_high, part_low = [], [], []

    def half_rows(value):
        return jnp.broadcast_to(value, (half_grid, 128))

    for i in range(cells.shape[0]):
        here = levels[:half_grid] == half_rows(row[i : i + 1])
        part_high.append(jnp.where(here, half_rows(high[i : i + 1]), zero[:half_grid]))
        part_low.append(jnp.where(here, half_rows(low[i : i + 1]), zero[:half_grid]))
        hit_column.append(jnp.where(levels == across(column[i : i + 1]), one, zero))
    left = jnp.concatenate(
        [jnp.concatenate(part_high, axis=1), jnp.concatenate(part_low, axis=1)], axis=0
    )
    right = jnp.concatenate(hit_column, axis=1)
    both = lax.dot_general(left, right, (((1,), (1,)), ((), ())), preferred_element_type=F32)
    return both[:half_grid] + both[half_grid:]


def lookup(cells, field, levels, row_levels):
    pair = cells >> 8
    place = (cells & 255).astype(F32).astype(BF16)
    zero, one = jnp.zeros((2 * GRID, 128), BF16), jnp.ones((2 * GRID, 128), BF16)
    half = GRID // 2
    value_x, value_y = [], []
    for first in range(0, cells.shape[0], 2):
        hits = [
            jnp.where(levels == jnp.broadcast_to(place[i : i + 1], (2 * GRID, 128)), one, zero)
            for i in (first, first + 1)
        ]
        picked = jnp.dot(field, jnp.concatenate(hits, axis=1), preferred_element_type=F32)
        for i in (0, 1):
            here = row_levels == jnp.broadcast_to(pair[first + i : first + i + 1], (half, 128))
            part = picked[:, 128 * i : 128 * (i + 1)]
            both_x = part[:half] + part[GRID : GRID + half]
            both_y = part[half:GRID] + part[GRID + half :]
            value_x.append(jnp.sum(jnp.where(here, both_x, 0.0), axis=0, keepdims=True))
            value_y.append(jnp.sum(jnp.where(here, both_y, 0.0), axis=0, keepdims=True))
    return jnp.concatenate(value_x, axis=0), jnp.concatenate(value_y, axis=0)


def reversed_block(block):
    lanes = 127 - lax.broadcasted_iota(jnp.int32, (8, 128), 1)
    rows = 7 - lax.broadcasted_iota(jnp.int32, (8, 128), 0)
    pieces = []
    for i in reversed(range(block.shape[0] // 8)):
        piece = jnp.take_along_axis(block[8 * i : 8 * i + 8], lanes, axis=1)
        pieces.append(jnp.take_along_axis(piece, rows, axis=0))
    return jnp.concatenate(pieces, axis=0)


def turn(state):
    pos_x, mom_x, pos_y, mom_y = state
    return (
        COS_X * pos_x + SIN_X * mom_x,
        -SIN_X * pos_x + COS_X * mom_x,
        COS_Y * pos_y + SIN_Y * mom_y,
        -SIN_Y * pos_y + COS_Y * mom_y,
    )


def kicked(base, kick_x, kick_y):
    return (
        base[0] + SIN_X * kick_x,
        base[1] + COS_X * kick_x,
        base[2] + SIN_Y * kick_y,
        base[3] + COS_Y * kick_y,
    )


def kernel(
    slices,
    particles,
    cells,
    counts_in,
    table,
    kept,
    arrived,
    arrived_kicks,
    state,
    cell,
    const,
    lefts,
    rights,
    counts,
    grid,
    scatter_in,
    half,
    window_in,
    spectrum,
    field,
    leavers,
    kicks,
    leaver_kicks,
    in_sem,
    scatter_sem,
    window_sem,
    share_sem,
    leave_sem,
    kick_sem,
):
    me = lax.axis_index("cuts")
    dom = lax.axis_index("dom")
    y_hi, core = dom // 2, dom % 2

    def behind(distance):
        return lax.rem(me + (distance + slices), slices)

    def member(y_flip, core_flip):
        y = 1 - y_hi if y_flip else y_hi
        c = 1 - core if core_flip else core
        return y * 2 + c

    def remote(src, dst, sems, index, cut, member_no):
        copy = pltpu.make_async_remote_copy(
            src_ref=src,
            dst_ref=dst,
            send_sem=sems.at[(0, *index)],
            recv_sem=sems.at[(1, *index)],
            device_id=(cut, member_no),
            device_id_type=MESH,
        )
        return copy

    ring = slices // 2
    place_in_ring = lax.rem(me, ring)
    lead = jnp.where(place_in_ring < ring // 2, 1, 0)
    use_first = lead
    second = jnp.where(place_in_ring >= ring // 2, 2, 3)
    loads = {}
    for turn_no in range(2):
        beam = lead if turn_no == 0 else 1 - lead
        loads["cells", turn_no] = pltpu.make_async_copy(
            cells.at[beam], cell.at[beam], in_sem.at[turn_no]
        )
        loads["weights", turn_no] = pltpu.make_async_copy(
            particles.at[beam, 4], state.at[beam, 4], in_sem.at[2 + turn_no]
        )
    for beam in (0, 1):
        loads["coords", beam] = pltpu.make_async_copy(
            particles.at[beam, pl.ds(0, 4)], state.at[beam, pl.ds(0, 4)], in_sem.at[4 + beam]
        )
    loads["table"] = pltpu.make_async_copy(table, const, in_sem.at[6])
    loads["counts"] = pltpu.make_async_copy(counts_in, counts, in_sem.at[7])
    for load in loads.values():
        load.start()

    barrier = pltpu.get_barrier_semaphore()
    partners = [(me, member(0, 1)), (me, member(1, 0)), (me, member(1, 1))]
    for distance in range(1, SECTIONS + 1):
        for sign in (1, -1):
            partners.append((behind(sign * distance), dom))
    for partner in partners:
        pl.semaphore_signal(barrier, inc=1, device_id=partner, device_id_type=MESH)

    pair_levels = lax.broadcasted_iota(jnp.int32, (2 * GRID, 128), 0).astype(F32).astype(BF16)
    levels = pair_levels[:GRID]
    row_levels = lax.broadcasted_iota(jnp.int32, (GRID // 2, 128), 0)
    def other_half_copies(beam):
        other = pl.ds(pl.multiple_of((1 - core) * 64, 64), 64)
        return [
            remote(
                grid.at[beam, other],
                scatter_in.at[beam, 2 * y_flip],
                scatter_sem,
                (beam, 2 * y_flip),
                me,
                member(y_flip, 1),
            )
            for y_flip in (1, 0)
        ]

    def own_half_copy(beam):
        mine = pl.ds(pl.multiple_of(core * 64, 64), 64)
        return remote(
            grid.at[beam, mine], scatter_in.at[beam, 1], scatter_sem, (beam, 1), me, member(1, 0)
        )

    def window_copies(beam):
        return [
            remote(
                half.at[beam],
                window_in.at[beam, distance - 1],
                window_sem,
                (beam, distance - 1),
                behind(distance * (1 - 2 * beam)),
                dom,
            )
            for distance in (2, 3, 1)
        ]

    def share_copy(beam):
        rows = pl.ds(pl.multiple_of(core * 64, 64), 64)
        place = spectrum.at[beam, rows]
        return remote(place, place, share_sem, (beam,), me, member(0, 1))

    def leave_copies(beam):
        return [
            remote(
                leavers.at[way, beam],
                arrived.at[beam, :, pl.ds(way * BLOCK, BLOCK)],
                leave_sem,
                (way, beam),
                behind(1 if way == 0 else -1),
                dom,
            )
            for way in range(2)
        ]

    def kick_copy(beam, way):
        return remote(
            leaver_kicks.at[beam, :, pl.ds((1 - way) * BLOCK, BLOCK)],
            arrived_kicks.at[beam, :, pl.ds(way * BLOCK, BLOCK)],
            kick_sem,
            (way, beam),
            behind(1 if way == 0 else -1),
            dom,
        )

    def start(copies):
        for copy in copies:
            copy.start()

    def window_send(beam):
        for copy in (*other_half_copies(beam), own_half_copy(beam)):
            copy.wait_recv()
        mine = pl.ds(pl.multiple_of(core * 64, 64), 64)
        half[beam] = (grid[beam, mine, :] + scatter_in[beam, 0]) + (
            scatter_in[beam, 1] + scatter_in[beam, 2]
        )
        start(window_copies(beam))

    def share_send(beam):
        for copy in window_copies(beam):
            copy.wait_recv()
        total = window_in[beam, 0]
        for distance in range(1, SECTIONS):
            total = total + window_in[beam, distance]
        rows = pl.ds(pl.multiple_of(core * 64, 64), 64)
        spectrum[beam, rows, :] = times_const(total, rights[:, :GRID])
        share_copy(beam).start()

    def solve(beam):
        share_copy(beam).wait_recv()
        scaled = const_times(lefts[:GRID, :], spectrum[beam]) * const[4]
        both = const_times(lefts[GRID:, :], scaled)
        field_x = times_const(both[:GRID], rights[:, :GRID])
        field_y = times_const(both[GRID:], rights[:, GRID:])
        half_grid = GRID // 2
        fields = jnp.concatenate(
            [
                jnp.concatenate([value[:half_grid], value[half_grid:]], axis=1)
                for value in (field_x, field_y)
            ],
            axis=0,
        )
        field[beam] = jnp.concatenate(parts(fields), axis=0)

    row_place = lax.broadcasted_iota(jnp.int32, (BLOCK, 128), 0) * 128 + lax.broadcasted_iota(
        jnp.int32, (BLOCK, 128), 1
    )
    def leaver_counts(beam):
        up = jnp.where(me == slices - 1, 0, counts[beam, 0, 0, 0])
        return up, jnp.where(me == 0, 0, counts[beam, 0, 0, 1])

    def leave_pack(beam):
        loads["coords", beam].wait()
        for way in range(2):
            rows = slice(ROWS - BLOCK, ROWS) if way == 0 else slice(0, BLOCK)
            limit = leaver_counts(beam)[way]
            base = turn([state[beam, comp, rows, :] for comp in range(4)])
            for comp, value in enumerate((*base, state[beam, 4, rows, :])):
                if way == 0:
                    value = reversed_block(value)
                leavers[way, beam, comp] = jnp.where(row_place < limit, value, 0.0)

    def look_up(beam, first, count):
        rows = pl.ds(pl.multiple_of(first, 8), count)
        kick_x, kick_y = lookup(cell[beam, rows, :], field[1 - beam], pair_levels, row_levels)
        kicks[beam, 0, rows, :] = kick_x
        kicks[beam, 1, rows, :] = kick_y
        shape = (count, 128)
        place = (first + lax.broadcasted_iota(jnp.int32, shape, 0)) * 128
        place = place + lax.broadcasted_iota(jnp.int32, shape, 1)
        stays = (place < ROWS * 128 - counts[beam, 0, 0, 0]) & (place >= counts[beam, 0, 0, 1])
        base = turn([state[beam, comp, rows, :] for comp in range(4)])
        for comp, value in enumerate((*kicked(base, kick_x, kick_y), state[beam, 4, rows, :])):
            kept[beam, comp, rows, :] = jnp.where(stays, value, 0.0)

    def kick_send(beam, way):
        limit = leaver_counts(beam)[way]
        rows = slice(ROWS - BLOCK, ROWS) if way == 0 else slice(0, BLOCK)
        place = slice((1 - way) * BLOCK, (2 - way) * BLOCK)
        for comp in range(2):
            kick = kicks[beam, comp, rows, :]
            if way == 0:
                kick = reversed_block(kick)
            leaver_kicks[beam, comp, place, :] = jnp.where(row_place < limit, kick, 0.0)
        kick_copy(beam, way).start()

    loads["cells", 0].wait()
    loads["weights", 0].wait()
    per_half = ROWS // DEPOSIT_ROWS
    per_beam = 2 * per_half

    def deposit_step(i, _):
        beam = jnp.where(i < per_beam, lead, 1 - lead)
        own = lax.rem(i // per_half, 2)
        inner = lax.rem(i, per_half)

        @pl.when(i == per_half + 1)
        def _():
            pl.semaphore_wait(barrier, len(partners))
            start(other_half_copies(lead))

        @pl.when(i == per_beam)
        def _():
            own_half_copy(lead).start()
            loads["cells", 1].wait()
            loads["weights", 1].wait()

        @pl.when(i == per_beam + per_half)
        def _():
            start(other_half_copies(1 - lead))

        rows = pl.ds(pl.multiple_of(inner * DEPOSIT_ROWS, DEPOSIT_ROWS), DEPOSIT_ROWS)
        first_row = jnp.where(own == 1, core, 1 - core) * 64
        place = pl.ds(pl.multiple_of(first_row, 64), 64)
        added = deposit(cell[beam, rows, :], state[beam, 4, rows, :], first_row, levels)

        @pl.when(inner == 0)
        def _():
            grid[beam, place, :] = added

        @pl.when(inner > 0)
        def _():
            grid[beam, place, :] = grid[beam, place, :] + added

        return 0

    lax.fori_loop(0, 2 * per_beam, deposit_step, 0)
    own_half_copy(1 - lead).start()
    loads["table"].wait()
    for i in range(3):
        lefts[pl.ds(i * GRID, GRID), :] = left_factor(const[i])
    rights[:, :GRID] = right_factor(const[0])
    rights[:, GRID:] = right_factor(const[3])
    window_send(lead)
    loads["counts"].wait()
    for beam in range(2):
        leave_pack(beam)
    window_send(1 - lead)
    share_send(use_first)
    for beam in range(2):
        start(leave_copies(beam))

    def look_step(i, _):
        now = jnp.where((i == second) | (i == second + 1) | (i > 5), use_first, 1 - use_first)
        block = jnp.where((i == 5) | (i == 7), 2, 1)
        block = jnp.where((i == 1) | (i == second + 1), 0, block)
        block = jnp.where((i == 0) | (i == second), 3, block)
        before = jnp.where(i > second, use_first, 1 - use_first)

        @pl.when((i == 0) | (i == second))
        def _():
            solve(1 - now)

        @pl.when(i == second - 1)
        def _():
            share_send(1 - use_first)

        @pl.when((i == 1) | (i == second + 1))
        def _():
            kick_send(before, 0)

        @pl.when((i == 2) | (i == second + 2))
        def _():
            kick_send(before, 1)

        look_up(now, block * BLOCK, BLOCK)
        return 0

    lax.fori_loop(0, 8, look_step, 0)
    for beam in range(2):
        for copy in (*leave_copies(beam), kick_copy(beam, 0), kick_copy(beam, 1)):
            copy.wait()
        scatter = (*other_half_copies(beam), own_half_copy(beam))
        for copy in (*scatter, *window_copies(beam), share_copy(beam)):
            copy.wait_send()


def finish(kept_in, arrived, arrived_kicks, kept, arrivals):
    for beam in range(2):
        kept[beam] = kept_in[beam]
        base = [arrived[beam, comp] for comp in range(4)]
        done = kicked(base, arrived_kicks[beam, 0], arrived_kicks[beam, 1])
        for comp, value in enumerate((*done, arrived[beam, 4])):
            arrivals[beam, comp] = value


def local(slices, particles, cells, counts):
    in_hbm = pl.BlockSpec(memory_space=pltpu.HBM)
    dma = pltpu.SemaphoreType.DMA
    in_vmem = pl.BlockSpec(memory_space=pltpu.VMEM)
    shapes = (
        jax.ShapeDtypeStruct((2, 5, ROWS, 128), F32),
        jax.ShapeDtypeStruct((2, 5, 2 * BLOCK, 128), F32),
    )
    results = pl.pallas_call(
        functools.partial(kernel, slices),
        out_shape=(*shapes, jax.ShapeDtypeStruct((2, 2, 2 * BLOCK, 128), F32)),
        in_specs=[
            in_hbm,
            in_hbm,
            in_hbm,
            in_hbm,
        ],
        out_specs=(in_vmem, in_vmem, in_vmem),
        scratch_shapes=[
            pltpu.VMEM((2, 5, ROWS, 128), F32),
            pltpu.VMEM((2, ROWS, 128), jnp.int32),
            pltpu.VMEM((5, GRID, GRID), F32),
            pltpu.VMEM((3 * GRID, 3 * GRID), BF16),
            pltpu.VMEM((3 * GRID, 2 * GRID), BF16),
            pltpu.SMEM((2, 1, 1, 2), jnp.int32),
            pltpu.VMEM((2, GRID, GRID), F32),
            pltpu.VMEM((2, 3, GRID // 2, GRID), F32),
            pltpu.VMEM((2, GRID // 2, GRID), F32),
            pltpu.VMEM((2, SECTIONS, GRID // 2, GRID), F32),
            pltpu.VMEM((2, GRID, GRID), F32),
            pltpu.VMEM((2, 2 * GRID, 2 * GRID), BF16),
            pltpu.VMEM((2, 2, 5, BLOCK, 128), F32),
            pltpu.VMEM((2, 2, ROWS, 128), F32),
            pltpu.VMEM((2, 2, 2 * BLOCK, 128), F32),
            dma((8,)),
            dma((2, 2, 3)),
            dma((2, 2, SECTIONS)),
            dma((2, 2)),
            dma((2, 2, 2)),
            dma((2, 2, 2)),
        ],
        compiler_params=pltpu.CompilerParams(
            collective_id=0, has_side_effects=True, vmem_limit_bytes=40 * 2**20
        ),
        cost_estimate=pl.CostEstimate(
            flops=7 * 10**9, bytes_accessed=2 * 10**6, transcendentals=0
        ),
        name="crossing",
    )(
        pltpu.with_memory_space_constraint(particles.reshape(2, 5, ROWS, 128), pltpu.HBM),
        pltpu.with_memory_space_constraint(cells.reshape(2, ROWS, 128), pltpu.HBM),
        pltpu.with_memory_space_constraint(counts.transpose(0, 2, 3, 1), pltpu.HBM),
        pltpu.with_memory_space_constraint(jnp.asarray(constants()), pltpu.HBM),
    )
    kept, arrivals = pl.pallas_call(
        finish,
        out_shape=shapes,
        in_specs=[in_vmem, in_vmem, in_vmem],
        out_specs=(in_vmem, in_vmem),
        name="finish",
    )(*(pltpu.with_memory_space_constraint(result, pltpu.VMEM) for result in results))
    return kept.reshape(2, 5, 1, ROWS * 128), arrivals.reshape(2, 5, 1, 2 * BLOCK * 128)


def solution(mesh):
    return jax.shard_map(
        functools.partial(local, mesh.shape["cuts"]),
        mesh=mesh,
        in_specs=(
            P(None, None, "cuts", "dom"),
            P(None, "cuts", "dom"),
            P(None, None, "cuts", "dom"),
        ),
        out_specs=(P(None, None, "cuts", "dom"), P(None, None, "cuts", "dom")),
        check_vma=False,
    )
```

```python
import functools
import math

import jax
import jax.numpy as jnp
import numpy as np
from jax import lax
from jax.experimental import pallas as pl
from jax.experimental.pallas import tpu as pltpu
from jax.sharding import PartitionSpec as P

MESH = pl.DeviceIdType.MESH
GRID = 128
SECTIONS = 3
ROWS = 128
BLOCK = 32
DEPOSIT_ROWS = 64
KICK_SCALE = 0.01
COS_X, SIN_X = (math.cos(2 * math.pi * 0.31), math.sin(2 * math.pi * 0.31))
COS_Y, SIN_Y = (math.cos(2 * math.pi * 0.32), math.sin(2 * math.pi * 0.32))
F32, BF16 = jnp.float32, jnp.bfloat16


def parts(values):
    high = values.astype(BF16)
    return high, (values - high.astype(F32)).astype(BF16)


def left_factor(a):
    high, low = parts(a)
    return jnp.concatenate([high, high, low], axis=1)


def right_factor(b):
    high, low = parts(b)
    return jnp.concatenate([high, low, high], axis=0)


def constants():
    index = np.arange(1, GRID + 1)
    angle = (index[:, None] * index[None, :] % (2 * (GRID + 1))) * (np.pi / (GRID + 1))
    basis = math.sqrt(2.0 / (GRID + 1)) * np.sin(angle)
    padded = np.pad(basis, ((1, 1), (0, 0)))
    slope = (padded[:-2] - padded[2:]) * (0.5 * KICK_SCALE)
    eigen = 2.0 - 2.0 * np.cos(index * (np.pi / (GRID + 1)))
    inverse = 1.0 / (eigen[:, None] + eigen[None, :])
    order = np.concatenate([np.arange(0, GRID, 2), np.arange(1, GRID, 2)])
    return np.stack([basis, slope[order], basis[order], slope.T, inverse]).astype(np.float32)


def times_const(a, right):
    return jnp.dot(left_factor(a), right, preferred_element_type=F32)


def const_times(left, b):
    return jnp.dot(left, right_factor(b), preferred_element_type=F32)


def across(row):
    return jnp.broadcast_to(row, (GRID, 128))


def deposit(cells, weights, first_row, levels):
    half_grid = GRID // 2
    row = ((cells >> 7) - first_row).astype(F32).astype(BF16)
    column = (cells & 127).astype(F32).astype(BF16)
    high, low = parts(weights)
    zero, one = jnp.zeros((GRID, 128), BF16), jnp.ones((GRID, 128), BF16)
    hit_column, part_high, part_low = [], [], []

    def half_rows(value):
        return jnp.broadcast_to(value, (half_grid, 128))

    for i in range(cells.shape[0]):
        here = levels[:half_grid] == half_rows(row[i : i + 1])
        part_high.append(jnp.where(here, half_rows(high[i : i + 1]), zero[:half_grid]))
        part_low.append(jnp.where(here, half_rows(low[i : i + 1]), zero[:half_grid]))
        hit_column.append(jnp.where(levels == across(column[i : i + 1]), one, zero))
    left = jnp.concatenate(
        [jnp.concatenate(part_high, axis=1), jnp.concatenate(part_low, axis=1)], axis=0
    )
    right = jnp.concatenate(hit_column, axis=1)
    both = lax.dot_general(left, right, (((1,), (1,)), ((), ())), preferred_element_type=F32)
    return both[:half_grid] + both[half_grid:]


def lookup(cells, field, levels, row_levels):
    pair = cells >> 8
    place = (cells & 255).astype(F32).astype(BF16)
    zero, one = jnp.zeros((2 * GRID, 128), BF16), jnp.ones((2 * GRID, 128), BF16)
    half = GRID // 2
    value_x, value_y = [], []
    for first in range(0, cells.shape[0], 2):
        hits = [
            jnp.where(levels == jnp.broadcast_to(place[i : i + 1], (2 * GRID, 128)), one, zero)
            for i in (first, first + 1)
        ]
        picked = jnp.dot(field, jnp.concatenate(hits, axis=1), preferred_element_type=F32)
        for i in (0, 1):
            here = row_levels == jnp.broadcast_to(pair[first + i : first + i + 1], (half, 128))
            part = picked[:, 128 * i : 128 * (i + 1)]
            both_x = part[:half] + part[GRID : GRID + half]
            both_y = part[half:GRID] + part[GRID + half :]
            value_x.append(jnp.sum(jnp.where(here, both_x, 0.0), axis=0, keepdims=True))
            value_y.append(jnp.sum(jnp.where(here, both_y, 0.0), axis=0, keepdims=True))
    return jnp.concatenate(value_x, axis=0), jnp.concatenate(value_y, axis=0)


def reversed_block(block):
    lanes = 127 - lax.broadcasted_iota(jnp.int32, (8, 128), 1)
    rows = 7 - lax.broadcasted_iota(jnp.int32, (8, 128), 0)
    pieces = []
    for i in reversed(range(block.shape[0] // 8)):
        piece = jnp.take_along_axis(block[8 * i : 8 * i + 8], lanes, axis=1)
        pieces.append(jnp.take_along_axis(piece, rows, axis=0))
    return jnp.concatenate(pieces, axis=0)


def turn(state):
    pos_x, mom_x, pos_y, mom_y = state
    return (
        COS_X * pos_x + SIN_X * mom_x,
        -SIN_X * pos_x + COS_X * mom_x,
        COS_Y * pos_y + SIN_Y * mom_y,
        -SIN_Y * pos_y + COS_Y * mom_y,
    )


def kicked(base, kick_x, kick_y):
    return (
        base[0] + SIN_X * kick_x,
        base[1] + COS_X * kick_x,
        base[2] + SIN_Y * kick_y,
        base[3] + COS_Y * kick_y,
    )


def kernel(
    slices,
    particles,
    cells,
    counts_in,
    table,
    kept,
    arrived,
    arrived_kicks,
    state,
    cell,
    const,
    lefts,
    rights,
    counts,
    grid,
    scatter_in,
    half,
    window_in,
    spectrum,
    field,
    leavers,
    kicks,
    leaver_kicks,
    in_sem,
    scatter_sem,
    window_sem,
    share_sem,
    leave_sem,
    kick_sem,
):
    me = lax.axis_index("cuts")
    dom = lax.axis_index("dom")
    y_hi, core = dom // 2, dom % 2

    def behind(distance):
        return lax.rem(me + (distance + slices), slices)

    def member(y_flip, core_flip):
        y = 1 - y_hi if y_flip else y_hi
        c = 1 - core if core_flip else core
        return y * 2 + c

    def remote(src, dst, sems, index, cut, member_no):
        copy = pltpu.make_async_remote_copy(
            src_ref=src,
            dst_ref=dst,
            send_sem=sems.at[(0, *index)],
            recv_sem=sems.at[(1, *index)],
            device_id=(cut, member_no),
            device_id_type=MESH,
        )
        return copy

    ring = slices // 2
    place_in_ring = lax.rem(me, ring)
    lead = jnp.where(place_in_ring < ring // 2, 1, 0)
    use_first = lead
    second = jnp.where(place_in_ring >= 0, 2, 3)
    loads = {}
    for turn_no in range(2):
        beam = lead if turn_no == 0 else 1 - lead
        loads["cells", turn_no] = pltpu.make_async_copy(
            cells.at[beam], cell.at[beam], in_sem.at[turn_no]
        )
        loads["weights", turn_no] = pltpu.make_async_copy(
            particles.at[beam, 4], state.at[beam, 4], in_sem.at[2 + turn_no]
        )
    for beam in (0, 1):
        loads["coords", beam] = pltpu.make_async_copy(
            particles.at[beam, pl.ds(0, 4)], state.at[beam, pl.ds(0, 4)], in_sem.at[4 + beam]
        )
    loads["table"] = pltpu.make_async_copy(table, const, in_sem.at[6])
    loads["counts"] = pltpu.make_async_copy(counts_in, counts, in_sem.at[7])
    for load in loads.values():
        load.start()

    barrier = pltpu.get_barrier_semaphore()
    partners = [(me, member(0, 1)), (me, member(1, 0)), (me, member(1, 1))]
    for distance in range(1, SECTIONS + 1):
        for sign in (1, -1):
            partners.append((behind(sign * distance), dom))
    for partner in partners:
        pl.semaphore_signal(barrier, inc=1, device_id=partner, device_id_type=MESH)

    pair_levels = lax.broadcasted_iota(jnp.int32, (2 * GRID, 128), 0).astype(F32).astype(BF16)
    levels = pair_levels[:GRID]
    row_levels = lax.broadcasted_iota(jnp.int32, (GRID // 2, 128), 0)
    def other_half_copies(beam):
        other = pl.ds(pl.multiple_of((1 - core) * 64, 64), 64)
        return [
            remote(
                grid.at[beam, other],
                scatter_in.at[beam, 2 * y_flip],
                scatter_sem,
                (beam, 2 * y_flip),
                me,
                member(y_flip, 1),
            )
            for y_flip in (1, 0)
        ]

    def own_half_copy(beam):
        mine = pl.ds(pl.multiple_of(core * 64, 64), 64)
        return remote(
            grid.at[beam, mine], scatter_in.at[beam, 1], scatter_sem, (beam, 1), me, member(1, 0)
        )

    def window_copies(beam):
        return [
            remote(
                half.at[beam],
                window_in.at[beam, distance - 1],
                window_sem,
                (beam, distance - 1),
                behind(distance * (1 - 2 * beam)),
                dom,
            )
            for distance in (2, 3, 1)
        ]

    def share_copy(beam):
        rows = pl.ds(pl.multiple_of(core * 64, 64), 64)
        place = spectrum.at[beam, rows]
        return remote(place, place, share_sem, (beam,), me, member(0, 1))

    def leave_copies(beam):
        return [
            remote(
                leavers.at[way, beam],
                arrived.at[beam, :, pl.ds(way * BLOCK, BLOCK)],
                leave_sem,
                (way, beam),
                behind(1 if way == 0 else -1),
                dom,
            )
            for way in range(2)
        ]

    def kick_copy(beam, way):
        return remote(
            leaver_kicks.at[beam, :, pl.ds((1 - way) * BLOCK, BLOCK)],
            arrived_kicks.at[beam, :, pl.ds(way * BLOCK, BLOCK)],
            kick_sem,
            (way, beam),
            behind(1 if way == 0 else -1),
            dom,
        )

    def start(copies):
        for copy in copies:
            copy.start()

    def window_send(beam):
        for copy in (*other_half_copies(beam), own_half_copy(beam)):
            copy.wait_recv()
        mine = pl.ds(pl.multiple_of(core * 64, 64), 64)
        half[beam] = (grid[beam, mine, :] + scatter_in[beam, 0]) + (
            scatter_in[beam, 1] + scatter_in[beam, 2]
        )
        start(window_copies(beam))

    def share_send(beam):
        for copy in window_copies(beam):
            copy.wait_recv()
        total = window_in[beam, 0]
        for distance in range(1, SECTIONS):
            total = total + window_in[beam, distance]
        rows = pl.ds(pl.multiple_of(core * 64, 64), 64)
        spectrum[beam, rows, :] = times_const(total, rights[:, :GRID])
        share_copy(beam).start()

    def solve(beam):
        share_copy(beam).wait_recv()
        scaled = const_times(lefts[:GRID, :], spectrum[beam]) * const[4]
        both = const_times(lefts[GRID:, :], scaled)
        field_x = times_const(both[:GRID], rights[:, :GRID])
        field_y = times_const(both[GRID:], rights[:, GRID:])
        half_grid = GRID // 2
        fields = jnp.concatenate(
            [
                jnp.concatenate([value[:half_grid], value[half_grid:]], axis=1)
                for value in (field_x, field_y)
            ],
            axis=0,
        )
        field[beam] = jnp.concatenate(parts(fields), axis=0)

    row_place = lax.broadcasted_iota(jnp.int32, (BLOCK, 128), 0) * 128 + lax.broadcasted_iota(
        jnp.int32, (BLOCK, 128), 1
    )
    def leaver_counts(beam):
        up = jnp.where(me == slices - 1, 0, counts[beam, 0, 0, 0])
        return up, jnp.where(me == 0, 0, counts[beam, 0, 0, 1])

    def leave_pack(beam):
        loads["coords", beam].wait()
        for way in range(2):
            rows = slice(ROWS - BLOCK, ROWS) if way == 0 else slice(0, BLOCK)
            limit = leaver_counts(beam)[way]
            base = turn([state[beam, comp, rows, :] for comp in range(4)])
            for comp, value in enumerate((*base, state[beam, 4, rows, :])):
                if way == 0:
                    value = reversed_block(value)
                leavers[way, beam, comp] = jnp.where(row_place < limit, value, 0.0)

    def look_up(beam, first, count):
        rows = pl.ds(pl.multiple_of(first, 8), count)
        kick_x, kick_y = lookup(cell[beam, rows, :], field[1 - beam], pair_levels, row_levels)
        kicks[beam, 0, rows, :] = kick_x
        kicks[beam, 1, rows, :] = kick_y
        shape = (count, 128)
        place = (first + lax.broadcasted_iota(jnp.int32, shape, 0)) * 128
        place = place + lax.broadcasted_iota(jnp.int32, shape, 1)
        stays = (place < ROWS * 128 - counts[beam, 0, 0, 0]) & (place >= counts[beam, 0, 0, 1])
        base = turn([state[beam, comp, rows, :] for comp in range(4)])
        for comp, value in enumerate((*kicked(base, kick_x, kick_y), state[beam, 4, rows, :])):
            kept[beam, comp, rows, :] = jnp.where(stays, value, 0.0)

    def kick_send(beam, way):
        limit = leaver_counts(beam)[way]
        rows = slice(ROWS - BLOCK, ROWS) if way == 0 else slice(0, BLOCK)
        place = slice((1 - way) * BLOCK, (2 - way) * BLOCK)
        for comp in range(2):
            kick = kicks[beam, comp, rows, :]
            if way == 0:
                kick = reversed_block(kick)
            leaver_kicks[beam, comp, place, :] = jnp.where(row_place < limit, kick, 0.0)
        kick_copy(beam, way).start()

    loads["cells", 0].wait()
    loads["weights", 0].wait()
    per_half = ROWS // DEPOSIT_ROWS
    per_beam = 2 * per_half

    def deposit_step(i, _):
        beam = jnp.where(i < per_beam, lead, 1 - lead)
        own = lax.rem(i // per_half, 2)
        inner = lax.rem(i, per_half)

        @pl.when(i == per_half + 1)
        def _():
            pl.semaphore_wait(barrier, len(partners))
            start(other_half_copies(lead))

        @pl.when(i == per_beam)
        def _():
            own_half_copy(lead).start()
            loads["cells", 1].wait()
            loads["weights", 1].wait()

        @pl.when(i == per_beam + per_half)
        def _():
            start(other_half_copies(1 - lead))

        rows = pl.ds(pl.multiple_of(inner * DEPOSIT_ROWS, DEPOSIT_ROWS), DEPOSIT_ROWS)
        first_row = jnp.where(own == 1, core, 1 - core) * 64
        place = pl.ds(pl.multiple_of(first_row, 64), 64)
        added = deposit(cell[beam, rows, :], state[beam, 4, rows, :], first_row, levels)

        @pl.when(inner == 0)
        def _():
            grid[beam, place, :] = added

        @pl.when(inner > 0)
        def _():
            grid[beam, place, :] = grid[beam, place, :] + added

        return 0

    lax.fori_loop(0, 2 * per_beam, deposit_step, 0)
    own_half_copy(1 - lead).start()
    loads["table"].wait()
    for i in range(3):
        lefts[pl.ds(i * GRID, GRID), :] = left_factor(const[i])
    rights[:, :GRID] = right_factor(const[0])
    rights[:, GRID:] = right_factor(const[3])
    window_send(lead)
    loads["counts"].wait()
    for beam in range(2):
        leave_pack(beam)
    window_send(1 - lead)
    share_send(use_first)
    for beam in range(2):
        start(leave_copies(beam))

    def look_step(i, _):
        now = jnp.where((i == second) | (i == second + 1) | (i > 5), use_first, 1 - use_first)
        block = jnp.where((i == 5) | (i == 7), 2, 1)
        block = jnp.where((i == 1) | (i == second + 1), 0, block)
        block = jnp.where((i == 0) | (i == second), 3, block)
        before = jnp.where(i > second, use_first, 1 - use_first)

        @pl.when((i == 0) | (i == second))
        def _():
            solve(1 - now)

        @pl.when(i == second - 1)
        def _():
            share_send(1 - use_first)

        @pl.when((i == 1) | (i == second + 1))
        def _():
            kick_send(before, 0)

        @pl.when((i == 2) | (i == second + 2))
        def _():
            kick_send(before, 1)

        look_up(now, block * BLOCK, BLOCK)
        return 0

    lax.fori_loop(0, 5, look_step, 0)

    @pl.when(second == 3)
    def _():
        kick_send(use_first, 1)

    look_up(1 - use_first, 2 * BLOCK, BLOCK)
    look_up(use_first, BLOCK, 2 * BLOCK)
    for beam in range(2):
        for copy in (*leave_copies(beam), kick_copy(beam, 0), kick_copy(beam, 1)):
            copy.wait()
        scatter = (*other_half_copies(beam), own_half_copy(beam))
        for copy in (*scatter, *window_copies(beam), share_copy(beam)):
            copy.wait_send()


def finish(kept_in, arrived, arrived_kicks, kept, arrivals):
    for beam in range(2):
        kept[beam] = kept_in[beam]
        base = [arrived[beam, comp] for comp in range(4)]
        done = kicked(base, arrived_kicks[beam, 0], arrived_kicks[beam, 1])
        for comp, value in enumerate((*done, arrived[beam, 4])):
            arrivals[beam, comp] = value


def local(slices, particles, cells, counts):
    in_hbm = pl.BlockSpec(memory_space=pltpu.HBM)
    dma = pltpu.SemaphoreType.DMA
    in_vmem = pl.BlockSpec(memory_space=pltpu.VMEM)
    shapes = (
        jax.ShapeDtypeStruct((2, 5, ROWS, 128), F32),
        jax.ShapeDtypeStruct((2, 5, 2 * BLOCK, 128), F32),
    )
    results = pl.pallas_call(
        functools.partial(kernel, slices),
        out_shape=(*shapes, jax.ShapeDtypeStruct((2, 2, 2 * BLOCK, 128), F32)),
        in_specs=[
            in_hbm,
            in_hbm,
            in_hbm,
            in_hbm,
        ],
        out_specs=(in_vmem, in_vmem, in_vmem),
        scratch_shapes=[
            pltpu.VMEM((2, 5, ROWS, 128), F32),
            pltpu.VMEM((2, ROWS, 128), jnp.int32),
            pltpu.VMEM((5, GRID, GRID), F32),
            pltpu.VMEM((3 * GRID, 3 * GRID), BF16),
            pltpu.VMEM((3 * GRID, 2 * GRID), BF16),
            pltpu.SMEM((2, 1, 1, 2), jnp.int32),
            pltpu.VMEM((2, GRID, GRID), F32),
            pltpu.VMEM((2, 3, GRID // 2, GRID), F32),
            pltpu.VMEM((2, GRID // 2, GRID), F32),
            pltpu.VMEM((2, SECTIONS, GRID // 2, GRID), F32),
            pltpu.VMEM((2, GRID, GRID), F32),
            pltpu.VMEM((2, 2 * GRID, 2 * GRID), BF16),
            pltpu.VMEM((2, 2, 5, BLOCK, 128), F32),
            pltpu.VMEM((2, 2, ROWS, 128), F32),
            pltpu.VMEM((2, 2, 2 * BLOCK, 128), F32),
            dma((8,)),
            dma((2, 2, 3)),
            dma((2, 2, SECTIONS)),
            dma((2, 2)),
            dma((2, 2, 2)),
            dma((2, 2, 2)),
        ],
        compiler_params=pltpu.CompilerParams(
            collective_id=0, has_side_effects=True, vmem_limit_bytes=40 * 2**20
        ),
        cost_estimate=pl.CostEstimate(
            flops=7 * 10**9, bytes_accessed=2 * 10**6, transcendentals=0
        ),
        name="crossing",
    )(
        pltpu.with_memory_space_constraint(particles.reshape(2, 5, ROWS, 128), pltpu.HBM),
        pltpu.with_memory_space_constraint(cells.reshape(2, ROWS, 128), pltpu.HBM),
        pltpu.with_memory_space_constraint(counts.transpose(0, 2, 3, 1), pltpu.HBM),
        pltpu.with_memory_space_constraint(jnp.asarray(constants()), pltpu.HBM),
    )
    kept, arrivals = pl.pallas_call(
        finish,
        out_shape=shapes,
        in_specs=[in_vmem, in_vmem, in_vmem],
        out_specs=(in_vmem, in_vmem),
        name="finish",
    )(*(pltpu.with_memory_space_constraint(result, pltpu.VMEM) for result in results))
    return kept.reshape(2, 5, 1, ROWS * 128), arrivals.reshape(2, 5, 1, 2 * BLOCK * 128)


def solution(mesh):
    return jax.shard_map(
        functools.partial(local, mesh.shape["cuts"]),
        mesh=mesh,
        in_specs=(
            P(None, None, "cuts", "dom"),
            P(None, "cuts", "dom"),
            P(None, None, "cuts", "dom"),
        ),
        out_specs=(P(None, None, "cuts", "dom"), P(None, None, "cuts", "dom")),
        check_vma=False,
    )
```

```python
import functools
import math

import jax
import jax.numpy as jnp
import numpy as np
from jax import lax
from jax.experimental import pallas as pl
from jax.experimental.pallas import tpu as pltpu
from jax.sharding import PartitionSpec as P

MESH = pl.DeviceIdType.MESH
GRID = 128
SECTIONS = 3
ROWS = 128
BLOCK = 32
DEPOSIT_ROWS = 64
KICK_SCALE = 0.01
COS_X, SIN_X = (math.cos(2 * math.pi * 0.31), math.sin(2 * math.pi * 0.31))
COS_Y, SIN_Y = (math.cos(2 * math.pi * 0.32), math.sin(2 * math.pi * 0.32))
F32, BF16 = jnp.float32, jnp.bfloat16


def parts(values):
    high = values.astype(BF16)
    return high, (values - high.astype(F32)).astype(BF16)


def left_factor(a):
    high, low = parts(a)
    return jnp.concatenate([high, high, low], axis=1)


def right_factor(b):
    high, low = parts(b)
    return jnp.concatenate([high, low, high], axis=0)


def constants():
    index = np.arange(1, GRID + 1)
    angle = (index[:, None] * index[None, :] % (2 * (GRID + 1))) * (np.pi / (GRID + 1))
    basis = math.sqrt(2.0 / (GRID + 1)) * np.sin(angle)
    padded = np.pad(basis, ((1, 1), (0, 0)))
    slope = (padded[:-2] - padded[2:]) * (0.5 * KICK_SCALE)
    eigen = 2.0 - 2.0 * np.cos(index * (np.pi / (GRID + 1)))
    inverse = 1.0 / (eigen[:, None] + eigen[None, :])
    order = np.concatenate([np.arange(0, GRID, 2), np.arange(1, GRID, 2)])
    return np.stack([basis, slope[order], basis[order], slope.T, inverse]).astype(np.float32)


def times_const(a, right):
    return jnp.dot(left_factor(a), right, preferred_element_type=F32)


def const_times(left, b):
    return jnp.dot(left, right_factor(b), preferred_element_type=F32)


def across(row):
    return jnp.broadcast_to(row, (GRID, 128))


def deposit(cells, weights, first_row, levels):
    half_grid = GRID // 2
    row = ((cells >> 7) - first_row).astype(F32).astype(BF16)
    column = (cells & 127).astype(F32).astype(BF16)
    high, low = parts(weights)
    zero, one = jnp.zeros((GRID, 128), BF16), jnp.ones((GRID, 128), BF16)
    hit_column, part_high, part_low = [], [], []

    def half_rows(value):
        return jnp.broadcast_to(value, (half_grid, 128))

    for i in range(cells.shape[0]):
        here = levels[:half_grid] == half_rows(row[i : i + 1])
        part_high.append(jnp.where(here, half_rows(high[i : i + 1]), zero[:half_grid]))
        part_low.append(jnp.where(here, half_rows(low[i : i + 1]), zero[:half_grid]))
        hit_column.append(jnp.where(levels == across(column[i : i + 1]), one, zero))
    left = jnp.concatenate(
        [jnp.concatenate(part_high, axis=1), jnp.concatenate(part_low, axis=1)], axis=0
    )
    right = jnp.concatenate(hit_column, axis=1)
    both = lax.dot_general(left, right, (((1,), (1,)), ((), ())), preferred_element_type=F32)
    return both[:half_grid] + both[half_grid:]


def lookup(cells, field, levels, row_levels):
    pair = cells >> 8
    place = (cells & 255).astype(F32).astype(BF16)
    zero, one = jnp.zeros((2 * GRID, 128), BF16), jnp.ones((2 * GRID, 128), BF16)
    half = GRID // 2
    value_x, value_y = [], []
    for first in range(0, cells.shape[0], 2):
        hits = [
            jnp.where(levels == jnp.broadcast_to(place[i : i + 1], (2 * GRID, 128)), one, zero)
            for i in (first, first + 1)
        ]
        picked = jnp.dot(field, jnp.concatenate(hits, axis=1), preferred_element_type=F32)
        for i in (0, 1):
            here = row_levels == jnp.broadcast_to(pair[first + i : first + i + 1], (half, 128))
            part = picked[:, 128 * i : 128 * (i + 1)]
            both_x = part[:half] + part[GRID : GRID + half]
            both_y = part[half:GRID] + part[GRID + half :]
            value_x.append(jnp.sum(jnp.where(here, both_x, 0.0), axis=0, keepdims=True))
            value_y.append(jnp.sum(jnp.where(here, both_y, 0.0), axis=0, keepdims=True))
    return jnp.concatenate(value_x, axis=0), jnp.concatenate(value_y, axis=0)


def reversed_block(block):
    lanes = 127 - lax.broadcasted_iota(jnp.int32, (8, 128), 1)
    rows = 7 - lax.broadcasted_iota(jnp.int32, (8, 128), 0)
    pieces = []
    for i in reversed(range(block.shape[0] // 8)):
        piece = jnp.take_along_axis(block[8 * i : 8 * i + 8], lanes, axis=1)
        pieces.append(jnp.take_along_axis(piece, rows, axis=0))
    return jnp.concatenate(pieces, axis=0)


def turn(state):
    pos_x, mom_x, pos_y, mom_y = state
    return (
        COS_X * pos_x + SIN_X * mom_x,
        -SIN_X * pos_x + COS_X * mom_x,
        COS_Y * pos_y + SIN_Y * mom_y,
        -SIN_Y * pos_y + COS_Y * mom_y,
    )


def kicked(base, kick_x, kick_y):
    return (
        base[0] + SIN_X * kick_x,
        base[1] + COS_X * kick_x,
        base[2] + SIN_Y * kick_y,
        base[3] + COS_Y * kick_y,
    )


def kernel(
    slices,
    particles,
    cells,
    counts_in,
    table,
    kept,
    arrived,
    arrived_kicks,
    state,
    cell,
    const,
    lefts,
    rights,
    counts,
    grid,
    scatter_in,
    half,
    window_in,
    spectrum,
    field,
    leavers,
    kicks,
    leaver_kicks,
    in_sem,
    scatter_sem,
    window_sem,
    share_sem,
    leave_sem,
    kick_sem,
):
    me = lax.axis_index("cuts")
    dom = lax.axis_index("dom")
    y_hi, core = dom // 2, dom % 2

    def behind(distance):
        return lax.rem(me + (distance + slices), slices)

    def member(y_flip, core_flip):
        y = 1 - y_hi if y_flip else y_hi
        c = 1 - core if core_flip else core
        return y * 2 + c

    def remote(src, dst, sems, index, cut, member_no):
        copy = pltpu.make_async_remote_copy(
            src_ref=src,
            dst_ref=dst,
            send_sem=sems.at[(0, *index)],
            recv_sem=sems.at[(1, *index)],
            device_id=(cut, member_no),
            device_id_type=MESH,
        )
        return copy

    ring = slices // 2
    place_in_ring = lax.rem(me, ring)
    lead = jnp.where(place_in_ring < ring // 2, 1, 0)
    use_first = lead
    second = jnp.where(place_in_ring >= 0, 2, 3)
    loads = {}
    for turn_no in range(2):
        beam = lead if turn_no == 0 else 1 - lead
        loads["cells", turn_no] = pltpu.make_async_copy(
            cells.at[beam], cell.at[beam], in_sem.at[turn_no]
        )
        loads["weights", turn_no] = pltpu.make_async_copy(
            particles.at[beam, 4], state.at[beam, 4], in_sem.at[2 + turn_no]
        )
    for beam in (0, 1):
        loads["coords", beam] = pltpu.make_async_copy(
            particles.at[beam, pl.ds(0, 4)], state.at[beam, pl.ds(0, 4)], in_sem.at[4 + beam]
        )
    loads["table"] = pltpu.make_async_copy(table, const, in_sem.at[6])
    loads["counts"] = pltpu.make_async_copy(counts_in, counts, in_sem.at[7])
    for load in loads.values():
        load.start()

    barrier = pltpu.get_barrier_semaphore()
    partners = [(me, member(0, 1)), (me, member(1, 0)), (me, member(1, 1))]
    for distance in range(1, SECTIONS + 1):
        for sign in (1, -1):
            partners.append((behind(sign * distance), dom))
    for partner in partners:
        pl.semaphore_signal(barrier, inc=1, device_id=partner, device_id_type=MESH)

    pair_levels = lax.broadcasted_iota(jnp.int32, (2 * GRID, 128), 0).astype(F32).astype(BF16)
    levels = pair_levels[:GRID]
    row_levels = lax.broadcasted_iota(jnp.int32, (GRID // 2, 128), 0)
    def other_half_copies(beam):
        other = pl.ds(pl.multiple_of((1 - core) * 64, 64), 64)
        return [
            remote(
                grid.at[beam, other],
                scatter_in.at[beam, 2 * y_flip],
                scatter_sem,
                (beam, 2 * y_flip),
                me,
                member(y_flip, 1),
            )
            for y_flip in (1, 0)
        ]

    def own_half_copy(beam):
        mine = pl.ds(pl.multiple_of(core * 64, 64), 64)
        return remote(
            grid.at[beam, mine], scatter_in.at[beam, 1], scatter_sem, (beam, 1), me, member(1, 0)
        )

    def window_copies(beam):
        return [
            remote(
                half.at[beam],
                window_in.at[beam, distance - 1],
                window_sem,
                (beam, distance - 1),
                behind(distance * (1 - 2 * beam)),
                dom,
            )
            for distance in (1, 3, 2)
        ]

    def share_copy(beam):
        rows = pl.ds(pl.multiple_of(core * 64, 64), 64)
        place = spectrum.at[beam, rows]
        return remote(place, place, share_sem, (beam,), me, member(0, 1))

    def leave_copies(beam):
        return [
            remote(
                leavers.at[way, beam],
                arrived.at[beam, :, pl.ds(way * BLOCK, BLOCK)],
                leave_sem,
                (way, beam),
                behind(1 if way == 0 else -1),
                dom,
            )
            for way in range(2)
        ]

    def kick_copy(beam, way):
        return remote(
            leaver_kicks.at[beam, :, pl.ds((1 - way) * BLOCK, BLOCK)],
            arrived_kicks.at[beam, :, pl.ds(way * BLOCK, BLOCK)],
            kick_sem,
            (way, beam),
            behind(1 if way == 0 else -1),
            dom,
        )

    def start(copies):
        for copy in copies:
            copy.start()

    def window_send(beam):
        for copy in (*other_half_copies(beam), own_half_copy(beam)):
            copy.wait_recv()
        mine = pl.ds(pl.multiple_of(core * 64, 64), 64)
        half[beam] = (grid[beam, mine, :] + scatter_in[beam, 0]) + (
            scatter_in[beam, 1] + scatter_in[beam, 2]
        )
        start(window_copies(beam))

    def share_send(beam):
        for copy in window_copies(beam):
            copy.wait_recv()
        total = window_in[beam, 0]
        for distance in range(1, SECTIONS):
            total = total + window_in[beam, distance]
        rows = pl.ds(pl.multiple_of(core * 64, 64), 64)
        spectrum[beam, rows, :] = times_const(total, rights[:, :GRID])
        share_copy(beam).start()

    def solve(beam):
        share_copy(beam).wait_recv()
        scaled = const_times(lefts[:GRID, :], spectrum[beam]) * const[4]
        both = const_times(lefts[GRID:, :], scaled)
        field_x = times_const(both[:GRID], rights[:, :GRID])
        field_y = times_const(both[GRID:], rights[:, GRID:])
        half_grid = GRID // 2
        fields = jnp.concatenate(
            [
                jnp.concatenate([value[:half_grid], value[half_grid:]], axis=1)
                for value in (field_x, field_y)
            ],
            axis=0,
        )
        field[beam] = jnp.concatenate(parts(fields), axis=0)

    row_place = lax.broadcasted_iota(jnp.int32, (BLOCK, 128), 0) * 128 + lax.broadcasted_iota(
        jnp.int32, (BLOCK, 128), 1
    )
    def leaver_counts(beam):
        up = jnp.where(me == slices - 1, 0, counts[beam, 0, 0, 0])
        return up, jnp.where(me == 0, 0, counts[beam, 0, 0, 1])

    def leave_pack(beam):
        loads["coords", beam].wait()
        for way in range(2):
            rows = slice(ROWS - BLOCK, ROWS) if way == 0 else slice(0, BLOCK)
            limit = leaver_counts(beam)[way]
            base = turn([state[beam, comp, rows, :] for comp in range(4)])
            for comp, value in enumerate((*base, state[beam, 4, rows, :])):
                if way == 0:
                    value = reversed_block(value)
                leavers[way, beam, comp] = jnp.where(row_place < limit, value, 0.0)

    def look_up(beam, first, count):
        rows = pl.ds(pl.multiple_of(first, 8), count)
        kick_x, kick_y = lookup(cell[beam, rows, :], field[1 - beam], pair_levels, row_levels)
        kicks[beam, 0, rows, :] = kick_x
        kicks[beam, 1, rows, :] = kick_y
        shape = (count, 128)
        place = (first + lax.broadcasted_iota(jnp.int32, shape, 0)) * 128
        place = place + lax.broadcasted_iota(jnp.int32, shape, 1)
        stays = (place < ROWS * 128 - counts[beam, 0, 0, 0]) & (place >= counts[beam, 0, 0, 1])
        base = turn([state[beam, comp, rows, :] for comp in range(4)])
        for comp, value in enumerate((*kicked(base, kick_x, kick_y), state[beam, 4, rows, :])):
            kept[beam, comp, rows, :] = jnp.where(stays, value, 0.0)

    def kick_send(beam, way):
        limit = leaver_counts(beam)[way]
        rows = slice(ROWS - BLOCK, ROWS) if way == 0 else slice(0, BLOCK)
        place = slice((1 - way) * BLOCK, (2 - way) * BLOCK)
        for comp in range(2):
            kick = kicks[beam, comp, rows, :]
            if way == 0:
                kick = reversed_block(kick)
            leaver_kicks[beam, comp, place, :] = jnp.where(row_place < limit, kick, 0.0)
        kick_copy(beam, way).start()

    loads["cells", 0].wait()
    loads["weights", 0].wait()
    per_half = ROWS // DEPOSIT_ROWS
    per_beam = 2 * per_half

    def deposit_step(i, _):
        beam = jnp.where(i < per_beam, lead, 1 - lead)
        own = lax.rem(i // per_half, 2)
        inner = lax.rem(i, per_half)

        @pl.when(i == per_half + 1)
        def _():
            pl.semaphore_wait(barrier, len(partners))
            start(other_half_copies(lead))

        @pl.when(i == per_beam)
        def _():
            own_half_copy(lead).start()
            loads["cells", 1].wait()
            loads["weights", 1].wait()

        @pl.when(i == per_beam + per_half)
        def _():
            start(other_half_copies(1 - lead))

        rows = pl.ds(pl.multiple_of(inner * DEPOSIT_ROWS, DEPOSIT_ROWS), DEPOSIT_ROWS)
        first_row = jnp.where(own == 1, core, 1 - core) * 64
        place = pl.ds(pl.multiple_of(first_row, 64), 64)
        added = deposit(cell[beam, rows, :], state[beam, 4, rows, :], first_row, levels)

        @pl.when(inner == 0)
        def _():
            grid[beam, place, :] = added

        @pl.when(inner > 0)
        def _():
            grid[beam, place, :] = grid[beam, place, :] + added

        return 0

    lax.fori_loop(0, 2 * per_beam, deposit_step, 0)
    own_half_copy(1 - lead).start()
    loads["table"].wait()
    for i in range(3):
        lefts[pl.ds(i * GRID, GRID), :] = left_factor(const[i])
    rights[:, :GRID] = right_factor(const[0])
    rights[:, GRID:] = right_factor(const[3])
    window_send(lead)
    loads["counts"].wait()
    for beam in range(2):
        leave_pack(beam)
    window_send(1 - lead)
    share_send(use_first)
    for beam in range(2):
        start(leave_copies(beam))

    def look_step(i, _):
        now = jnp.where((i == second) | (i == second + 1) | (i > 5), use_first, 1 - use_first)
        block = jnp.where((i == 5) | (i == 7), 2, 1)
        block = jnp.where((i == 1) | (i == second + 1), 0, block)
        block = jnp.where((i == 0) | (i == second), 3, block)
        before = jnp.where(i > second, use_first, 1 - use_first)

        @pl.when((i == 0) | (i == second))
        def _():
            solve(1 - now)

        @pl.when(i == second - 1)
        def _():
            share_send(1 - use_first)

        @pl.when((i == 1) | (i == second + 1))
        def _():
            kick_send(before, 0)

        @pl.when((i == 2) | (i == second + 2))
        def _():
            kick_send(before, 1)

        look_up(now, block * BLOCK, BLOCK)
        return 0

    lax.fori_loop(0, 5, look_step, 0)

    @pl.when(second == 3)
    def _():
        kick_send(use_first, 1)

    look_up(1 - use_first, 2 * BLOCK, BLOCK)
    look_up(use_first, BLOCK, 2 * BLOCK)
    for beam in range(2):
        for copy in (*leave_copies(beam), kick_copy(beam, 0), kick_copy(beam, 1)):
            copy.wait()
        scatter = (*other_half_copies(beam), own_half_copy(beam))
        for copy in (*scatter, *window_copies(beam), share_copy(beam)):
            copy.wait_send()


def finish(kept_in, arrived, arrived_kicks, kept, arrivals):
    for beam in range(2):
        kept[beam] = kept_in[beam]
        base = [arrived[beam, comp] for comp in range(4)]
        done = kicked(base, arrived_kicks[beam, 0], arrived_kicks[beam, 1])
        for comp, value in enumerate((*done, arrived[beam, 4])):
            arrivals[beam, comp] = value


def local(slices, particles, cells, counts):
    in_hbm = pl.BlockSpec(memory_space=pltpu.HBM)
    dma = pltpu.SemaphoreType.DMA
    in_vmem = pl.BlockSpec(memory_space=pltpu.VMEM)
    shapes = (
        jax.ShapeDtypeStruct((2, 5, ROWS, 128), F32),
        jax.ShapeDtypeStruct((2, 5, 2 * BLOCK, 128), F32),
    )
    results = pl.pallas_call(
        functools.partial(kernel, slices),
        out_shape=(*shapes, jax.ShapeDtypeStruct((2, 2, 2 * BLOCK, 128), F32)),
        in_specs=[
            in_hbm,
            in_hbm,
            in_hbm,
            in_hbm,
        ],
        out_specs=(in_vmem, in_vmem, in_vmem),
        scratch_shapes=[
            pltpu.VMEM((2, 5, ROWS, 128), F32),
            pltpu.VMEM((2, ROWS, 128), jnp.int32),
            pltpu.VMEM((5, GRID, GRID), F32),
            pltpu.VMEM((3 * GRID, 3 * GRID), BF16),
            pltpu.VMEM((3 * GRID, 2 * GRID), BF16),
            pltpu.SMEM((2, 1, 1, 2), jnp.int32),
            pltpu.VMEM((2, GRID, GRID), F32),
            pltpu.VMEM((2, 3, GRID // 2, GRID), F32),
            pltpu.VMEM((2, GRID // 2, GRID), F32),
            pltpu.VMEM((2, SECTIONS, GRID // 2, GRID), F32),
            pltpu.VMEM((2, GRID, GRID), F32),
            pltpu.VMEM((2, 2 * GRID, 2 * GRID), BF16),
            pltpu.VMEM((2, 2, 5, BLOCK, 128), F32),
            pltpu.VMEM((2, 2, ROWS, 128), F32),
            pltpu.VMEM((2, 2, 2 * BLOCK, 128), F32),
            dma((8,)),
            dma((2, 2, 3)),
            dma((2, 2, SECTIONS)),
            dma((2, 2)),
            dma((2, 2, 2)),
            dma((2, 2, 2)),
        ],
        compiler_params=pltpu.CompilerParams(
            collective_id=0, has_side_effects=True, vmem_limit_bytes=40 * 2**20
        ),
        cost_estimate=pl.CostEstimate(
            flops=7 * 10**9, bytes_accessed=2 * 10**6, transcendentals=0
        ),
        name="crossing",
    )(
        pltpu.with_memory_space_constraint(particles.reshape(2, 5, ROWS, 128), pltpu.HBM),
        pltpu.with_memory_space_constraint(cells.reshape(2, ROWS, 128), pltpu.HBM),
        pltpu.with_memory_space_constraint(counts.transpose(0, 2, 3, 1), pltpu.HBM),
        pltpu.with_memory_space_constraint(jnp.asarray(constants()), pltpu.HBM),
    )
    kept, arrivals = pl.pallas_call(
        finish,
        out_shape=shapes,
        in_specs=[in_vmem, in_vmem, in_vmem],
        out_specs=(in_vmem, in_vmem),
        name="finish",
    )(*(pltpu.with_memory_space_constraint(result, pltpu.VMEM) for result in results))
    return kept.reshape(2, 5, 1, ROWS * 128), arrivals.reshape(2, 5, 1, 2 * BLOCK * 128)


def solution(mesh):
    return jax.shard_map(
        functools.partial(local, mesh.shape["cuts"]),
        mesh=mesh,
        in_specs=(
            P(None, None, "cuts", "dom"),
            P(None, "cuts", "dom"),
            P(None, None, "cuts", "dom"),
        ),
        out_specs=(P(None, None, "cuts", "dom"), P(None, None, "cuts", "dom")),
        check_vma=False,
    )
```

```python
import functools
import math

import jax
import jax.numpy as jnp
import numpy as np
from jax import lax
from jax.experimental import pallas as pl
from jax.experimental.pallas import tpu as pltpu
from jax.sharding import PartitionSpec as P

MESH = pl.DeviceIdType.MESH
GRID = 128
SECTIONS = 3
ROWS = 128
BLOCK = 32
DEPOSIT_ROWS = 64
KICK_SCALE = 0.01
COS_X, SIN_X = (math.cos(2 * math.pi * 0.31), math.sin(2 * math.pi * 0.31))
COS_Y, SIN_Y = (math.cos(2 * math.pi * 0.32), math.sin(2 * math.pi * 0.32))
F32, BF16 = jnp.float32, jnp.bfloat16


def parts(values):
    high = values.astype(BF16)
    return high, (values - high.astype(F32)).astype(BF16)


def left_factor(a):
    high, low = parts(a)
    return jnp.concatenate([high, high, low], axis=1)


def right_factor(b):
    high, low = parts(b)
    return jnp.concatenate([high, low, high], axis=0)


def constants():
    index = np.arange(1, GRID + 1)
    angle = (index[:, None] * index[None, :] % (2 * (GRID + 1))) * (np.pi / (GRID + 1))
    basis = math.sqrt(2.0 / (GRID + 1)) * np.sin(angle)
    padded = np.pad(basis, ((1, 1), (0, 0)))
    slope = (padded[:-2] - padded[2:]) * (0.5 * KICK_SCALE)
    eigen = 2.0 - 2.0 * np.cos(index * (np.pi / (GRID + 1)))
    inverse = 1.0 / (eigen[:, None] + eigen[None, :])
    order = np.concatenate([np.arange(0, GRID, 2), np.arange(1, GRID, 2)])
    return np.stack([basis, slope[order], basis[order], slope.T, inverse]).astype(np.float32)


def times_const(a, right):
    return jnp.dot(left_factor(a), right, preferred_element_type=F32)


def const_times(left, b):
    return jnp.dot(left, right_factor(b), preferred_element_type=F32)


def across(row):
    return jnp.broadcast_to(row, (GRID, 128))


def deposit(cells, weights, first_row, levels):
    half_grid = GRID // 2
    row = ((cells >> 7) - first_row).astype(F32).astype(BF16)
    column = (cells & 127).astype(F32).astype(BF16)
    high, low = parts(weights)
    zero, one = jnp.zeros((GRID, 128), BF16), jnp.ones((GRID, 128), BF16)
    hit_column, part_high, part_low = [], [], []

    def half_rows(value):
        return jnp.broadcast_to(value, (half_grid, 128))

    for i in range(cells.shape[0]):
        here = levels[:half_grid] == half_rows(row[i : i + 1])
        part_high.append(jnp.where(here, half_rows(high[i : i + 1]), zero[:half_grid]))
        part_low.append(jnp.where(here, half_rows(low[i : i + 1]), zero[:half_grid]))
        hit_column.append(jnp.where(levels == across(column[i : i + 1]), one, zero))
    left = jnp.concatenate(
        [jnp.concatenate(part_high, axis=1), jnp.concatenate(part_low, axis=1)], axis=0
    )
    right = jnp.concatenate(hit_column, axis=1)
    both = lax.dot_general(left, right, (((1,), (1,)), ((), ())), preferred_element_type=F32)
    return both[:half_grid] + both[half_grid:]


def lookup(cells, field, levels, row_levels):
    pair = cells >> 8
    place = (cells & 255).astype(F32).astype(BF16)
    zero, one = jnp.zeros((2 * GRID, 128), BF16), jnp.ones((2 * GRID, 128), BF16)
    half = GRID // 2
    value_x, value_y = [], []
    for first in range(0, cells.shape[0], 2):
        hits = [
            jnp.where(levels == jnp.broadcast_to(place[i : i + 1], (2 * GRID, 128)), one, zero)
            for i in (first, first + 1)
        ]
        picked = jnp.dot(field, jnp.concatenate(hits, axis=1), preferred_element_type=F32)
        for i in (0, 1):
            here = row_levels == jnp.broadcast_to(pair[first + i : first + i + 1], (half, 128))
            part = picked[:, 128 * i : 128 * (i + 1)]
            both_x = part[:half] + part[GRID : GRID + half]
            both_y = part[half:GRID] + part[GRID + half :]
            value_x.append(jnp.sum(jnp.where(here, both_x, 0.0), axis=0, keepdims=True))
            value_y.append(jnp.sum(jnp.where(here, both_y, 0.0), axis=0, keepdims=True))
    return jnp.concatenate(value_x, axis=0), jnp.concatenate(value_y, axis=0)


def reversed_block(block):
    lanes = 127 - lax.broadcasted_iota(jnp.int32, (8, 128), 1)
    rows = 7 - lax.broadcasted_iota(jnp.int32, (8, 128), 0)
    pieces = []
    for i in reversed(range(block.shape[0] // 8)):
        piece = jnp.take_along_axis(block[8 * i : 8 * i + 8], lanes, axis=1)
        pieces.append(jnp.take_along_axis(piece, rows, axis=0))
    return jnp.concatenate(pieces, axis=0)


def turn(state):
    pos_x, mom_x, pos_y, mom_y = state
    return (
        COS_X * pos_x + SIN_X * mom_x,
        -SIN_X * pos_x + COS_X * mom_x,
        COS_Y * pos_y + SIN_Y * mom_y,
        -SIN_Y * pos_y + COS_Y * mom_y,
    )


def kicked(base, kick_x, kick_y):
    return (
        base[0] + SIN_X * kick_x,
        base[1] + COS_X * kick_x,
        base[2] + SIN_Y * kick_y,
        base[3] + COS_Y * kick_y,
    )


def kernel(
    slices,
    particles,
    cells,
    counts_in,
    table,
    kept,
    arrived,
    arrived_kicks,
    state,
    cell,
    const,
    lefts,
    rights,
    counts,
    grid,
    scatter_in,
    half,
    window_in,
    spectrum,
    field,
    leavers,
    kicks,
    leaver_kicks,
    in_sem,
    scatter_sem,
    window_sem,
    share_sem,
    leave_sem,
    kick_sem,
):
    me = lax.axis_index("cuts")
    dom = lax.axis_index("dom")
    y_hi, core = dom // 2, dom % 2

    def behind(distance):
        return lax.rem(me + (distance + slices), slices)

    def member(y_flip, core_flip):
        y = 1 - y_hi if y_flip else y_hi
        c = 1 - core if core_flip else core
        return y * 2 + c

    def remote(src, dst, sems, index, cut, member_no):
        copy = pltpu.make_async_remote_copy(
            src_ref=src,
            dst_ref=dst,
            send_sem=sems.at[(0, *index)],
            recv_sem=sems.at[(1, *index)],
            device_id=(cut, member_no),
            device_id_type=MESH,
        )
        return copy

    ring = slices // 2
    place_in_ring = lax.rem(me, ring)
    lead = jnp.where(place_in_ring < ring // 2, 1, 0)
    use_first = lead
    second = jnp.where(place_in_ring >= 0, 2, 3)
    loads = {}
    for turn_no in range(2):
        beam = lead if turn_no == 0 else 1 - lead
        loads["cells", turn_no] = pltpu.make_async_copy(
            cells.at[beam], cell.at[beam], in_sem.at[turn_no]
        )
        loads["weights", turn_no] = pltpu.make_async_copy(
            particles.at[beam, 4], state.at[beam, 4], in_sem.at[2 + turn_no]
        )
    for beam in (0, 1):
        loads["coords", beam] = pltpu.make_async_copy(
            particles.at[beam, pl.ds(0, 4)], state.at[beam, pl.ds(0, 4)], in_sem.at[4 + beam]
        )
    loads["table"] = pltpu.make_async_copy(table, const, in_sem.at[6])
    loads["counts"] = pltpu.make_async_copy(counts_in, counts, in_sem.at[7])
    for load in loads.values():
        load.start()

    barrier = pltpu.get_barrier_semaphore()
    partners = [(me, member(0, 1)), (me, member(1, 0)), (me, member(1, 1))]
    for distance in range(1, SECTIONS + 1):
        for sign in (1, -1):
            partners.append((behind(sign * distance), dom))
    for partner in partners:
        pl.semaphore_signal(barrier, inc=1, device_id=partner, device_id_type=MESH)

    pair_levels = lax.broadcasted_iota(jnp.int32, (2 * GRID, 128), 0).astype(F32).astype(BF16)
    levels = pair_levels[:GRID]
    row_levels = lax.broadcasted_iota(jnp.int32, (GRID // 2, 128), 0)
    def other_half_copies(beam):
        other = pl.ds(pl.multiple_of((1 - core) * 64, 64), 64)
        return [
            remote(
                grid.at[beam, other],
                scatter_in.at[beam, 2 * y_flip],
                scatter_sem,
                (beam, 2 * y_flip),
                me,
                member(y_flip, 1),
            )
            for y_flip in (1, 0)
        ]

    def own_half_copy(beam):
        mine = pl.ds(pl.multiple_of(core * 64, 64), 64)
        return remote(
            grid.at[beam, mine], scatter_in.at[beam, 1], scatter_sem, (beam, 1), me, member(1, 0)
        )

    def window_copies(beam):
        return [
            remote(
                half.at[beam],
                window_in.at[beam, distance - 1],
                window_sem,
                (beam, distance - 1),
                behind(distance * (1 - 2 * beam)),
                dom,
            )
            for distance in (3, 1, 2)
        ]

    def share_copy(beam):
        rows = pl.ds(pl.multiple_of(core * 64, 64), 64)
        place = spectrum.at[beam, rows]
        return remote(place, place, share_sem, (beam,), me, member(0, 1))

    def leave_copies(beam):
        return [
            remote(
                leavers.at[way, beam],
                arrived.at[beam, :, pl.ds(way * BLOCK, BLOCK)],
                leave_sem,
                (way, beam),
                behind(1 if way == 0 else -1),
                dom,
            )
            for way in range(2)
        ]

    def kick_copy(beam, way):
        return remote(
            leaver_kicks.at[beam, :, pl.ds((1 - way) * BLOCK, BLOCK)],
            arrived_kicks.at[beam, :, pl.ds(way * BLOCK, BLOCK)],
            kick_sem,
            (way, beam),
            behind(1 if way == 0 else -1),
            dom,
        )

    def start(copies):
        for copy in copies:
            copy.start()

    def window_send(beam):
        for copy in (*other_half_copies(beam), own_half_copy(beam)):
            copy.wait_recv()
        mine = pl.ds(pl.multiple_of(core * 64, 64), 64)
        half[beam] = (grid[beam, mine, :] + scatter_in[beam, 0]) + (
            scatter_in[beam, 1] + scatter_in[beam, 2]
        )
        start(window_copies(beam))

    def share_send(beam):
        for copy in window_copies(beam):
            copy.wait_recv()
        total = window_in[beam, 0]
        for distance in range(1, SECTIONS):
            total = total + window_in[beam, distance]
        rows = pl.ds(pl.multiple_of(core * 64, 64), 64)
        spectrum[beam, rows, :] = times_const(total, rights[:, :GRID])
        share_copy(beam).start()

    def solve(beam):
        share_copy(beam).wait_recv()
        scaled = const_times(lefts[:GRID, :], spectrum[beam]) * const[4]
        both = const_times(lefts[GRID:, :], scaled)
        field_x = times_const(both[:GRID], rights[:, :GRID])
        field_y = times_const(both[GRID:], rights[:, GRID:])
        half_grid = GRID // 2
        fields = jnp.concatenate(
            [
                jnp.concatenate([value[:half_grid], value[half_grid:]], axis=1)
                for value in (field_x, field_y)
            ],
            axis=0,
        )
        field[beam] = jnp.concatenate(parts(fields), axis=0)

    row_place = lax.broadcasted_iota(jnp.int32, (BLOCK, 128), 0) * 128 + lax.broadcasted_iota(
        jnp.int32, (BLOCK, 128), 1
    )
    def leaver_counts(beam):
        up = jnp.where(me == slices - 1, 0, counts[beam, 0, 0, 0])
        return up, jnp.where(me == 0, 0, counts[beam, 0, 0, 1])

    def leave_pack(beam):
        loads["coords", beam].wait()
        for way in range(2):
            rows = slice(ROWS - BLOCK, ROWS) if way == 0 else slice(0, BLOCK)
            limit = leaver_counts(beam)[way]
            base = turn([state[beam, comp, rows, :] for comp in range(4)])
            for comp, value in enumerate((*base, state[beam, 4, rows, :])):
                if way == 0:
                    value = reversed_block(value)
                leavers[way, beam, comp] = jnp.where(row_place < limit, value, 0.0)

    def look_up(beam, first, count):
        rows = pl.ds(pl.multiple_of(first, 8), count)
        kick_x, kick_y = lookup(cell[beam, rows, :], field[1 - beam], pair_levels, row_levels)
        kicks[beam, 0, rows, :] = kick_x
        kicks[beam, 1, rows, :] = kick_y
        shape = (count, 128)
        place = (first + lax.broadcasted_iota(jnp.int32, shape, 0)) * 128
        place = place + lax.broadcasted_iota(jnp.int32, shape, 1)
        stays = (place < ROWS * 128 - counts[beam, 0, 0, 0]) & (place >= counts[beam, 0, 0, 1])
        base = turn([state[beam, comp, rows, :] for comp in range(4)])
        for comp, value in enumerate((*kicked(base, kick_x, kick_y), state[beam, 4, rows, :])):
            kept[beam, comp, rows, :] = jnp.where(stays, value, 0.0)

    def kick_send(beam, way):
        limit = leaver_counts(beam)[way]
        rows = slice(ROWS - BLOCK, ROWS) if way == 0 else slice(0, BLOCK)
        place = slice((1 - way) * BLOCK, (2 - way) * BLOCK)
        for comp in range(2):
            kick = kicks[beam, comp, rows, :]
            if way == 0:
                kick = reversed_block(kick)
            leaver_kicks[beam, comp, place, :] = jnp.where(row_place < limit, kick, 0.0)
        kick_copy(beam, way).start()

    loads["cells", 0].wait()
    loads["weights", 0].wait()
    per_half = ROWS // DEPOSIT_ROWS
    per_beam = 2 * per_half

    def deposit_step(i, _):
        beam = jnp.where(i < per_beam, lead, 1 - lead)
        own = lax.rem(i // per_half, 2)
        inner = lax.rem(i, per_half)

        @pl.when(i == per_half + 1)
        def _():
            pl.semaphore_wait(barrier, len(partners))
            start(other_half_copies(lead))

        @pl.when(i == per_beam)
        def _():
            own_half_copy(lead).start()
            loads["cells", 1].wait()
            loads["weights", 1].wait()

        @pl.when(i == per_beam + per_half)
        def _():
            start(other_half_copies(1 - lead))

        rows = pl.ds(pl.multiple_of(inner * DEPOSIT_ROWS, DEPOSIT_ROWS), DEPOSIT_ROWS)
        first_row = jnp.where(own == 1, core, 1 - core) * 64
        place = pl.ds(pl.multiple_of(first_row, 64), 64)
        added = deposit(cell[beam, rows, :], state[beam, 4, rows, :], first_row, levels)

        @pl.when(inner == 0)
        def _():
            grid[beam, place, :] = added

        @pl.when(inner > 0)
        def _():
            grid[beam, place, :] = grid[beam, place, :] + added

        return 0

    lax.fori_loop(0, 2 * per_beam, deposit_step, 0)
    own_half_copy(1 - lead).start()
    loads["table"].wait()
    for i in range(3):
        lefts[pl.ds(i * GRID, GRID), :] = left_factor(const[i])
    rights[:, :GRID] = right_factor(const[0])
    rights[:, GRID:] = right_factor(const[3])
    window_send(lead)
    loads["counts"].wait()
    for beam in range(2):
        leave_pack(beam)
    window_send(1 - lead)
    share_send(use_first)
    for beam in range(2):
        start(leave_copies(beam))

    def look_step(i, _):
        now = jnp.where((i == second) | (i == second + 1) | (i > 5), use_first, 1 - use_first)
        block = jnp.where((i == 5) | (i == 7), 2, 1)
        block = jnp.where((i == 1) | (i == second + 1), 0, block)
        block = jnp.where((i == 0) | (i == second), 3, block)
        before = jnp.where(i > second, use_first, 1 - use_first)

        @pl.when((i == 0) | (i == second))
        def _():
            solve(1 - now)

        @pl.when(i == second - 1)
        def _():
            share_send(1 - use_first)

        @pl.when((i == 1) | (i == second + 1))
        def _():
            kick_send(before, 0)

        @pl.when((i == 2) | (i == second + 2))
        def _():
            kick_send(before, 1)

        look_up(now, block * BLOCK, BLOCK)
        return 0

    lax.fori_loop(0, 5, look_step, 0)

    @pl.when(second == 3)
    def _():
        kick_send(use_first, 1)

    look_up(1 - use_first, 2 * BLOCK, BLOCK)
    look_up(use_first, BLOCK, 2 * BLOCK)
    for beam in range(2):
        for copy in (*leave_copies(beam), kick_copy(beam, 0), kick_copy(beam, 1)):
            copy.wait()
        scatter = (*other_half_copies(beam), own_half_copy(beam))
        for copy in (*scatter, *window_copies(beam), share_copy(beam)):
            copy.wait_send()


def finish(kept_in, arrived, arrived_kicks, kept, arrivals):
    for beam in range(2):
        kept[beam] = kept_in[beam]
        base = [arrived[beam, comp] for comp in range(4)]
        done = kicked(base, arrived_kicks[beam, 0], arrived_kicks[beam, 1])
        for comp, value in enumerate((*done, arrived[beam, 4])):
            arrivals[beam, comp] = value


def local(slices, particles, cells, counts):
    in_hbm = pl.BlockSpec(memory_space=pltpu.HBM)
    dma = pltpu.SemaphoreType.DMA
    in_vmem = pl.BlockSpec(memory_space=pltpu.VMEM)
    shapes = (
        jax.ShapeDtypeStruct((2, 5, ROWS, 128), F32),
        jax.ShapeDtypeStruct((2, 5, 2 * BLOCK, 128), F32),
    )
    results = pl.pallas_call(
        functools.partial(kernel, slices),
        out_shape=(*shapes, jax.ShapeDtypeStruct((2, 2, 2 * BLOCK, 128), F32)),
        in_specs=[
            in_hbm,
            in_hbm,
            in_hbm,
            in_hbm,
        ],
        out_specs=(in_vmem, in_vmem, in_vmem),
        scratch_shapes=[
            pltpu.VMEM((2, 5, ROWS, 128), F32),
            pltpu.VMEM((2, ROWS, 128), jnp.int32),
            pltpu.VMEM((5, GRID, GRID), F32),
            pltpu.VMEM((3 * GRID, 3 * GRID), BF16),
            pltpu.VMEM((3 * GRID, 2 * GRID), BF16),
            pltpu.SMEM((2, 1, 1, 2), jnp.int32),
            pltpu.VMEM((2, GRID, GRID), F32),
            pltpu.VMEM((2, 3, GRID // 2, GRID), F32),
            pltpu.VMEM((2, GRID // 2, GRID), F32),
            pltpu.VMEM((2, SECTIONS, GRID // 2, GRID), F32),
            pltpu.VMEM((2, GRID, GRID), F32),
            pltpu.VMEM((2, 2 * GRID, 2 * GRID), BF16),
            pltpu.VMEM((2, 2, 5, BLOCK, 128), F32),
            pltpu.VMEM((2, 2, ROWS, 128), F32),
            pltpu.VMEM((2, 2, 2 * BLOCK, 128), F32),
            dma((8,)),
            dma((2, 2, 3)),
            dma((2, 2, SECTIONS)),
            dma((2, 2)),
            dma((2, 2, 2)),
            dma((2, 2, 2)),
        ],
        compiler_params=pltpu.CompilerParams(
            collective_id=0, has_side_effects=True, vmem_limit_bytes=40 * 2**20
        ),
        cost_estimate=pl.CostEstimate(
            flops=7 * 10**9, bytes_accessed=2 * 10**6, transcendentals=0
        ),
        name="crossing",
    )(
        pltpu.with_memory_space_constraint(particles.reshape(2, 5, ROWS, 128), pltpu.HBM),
        pltpu.with_memory_space_constraint(cells.reshape(2, ROWS, 128), pltpu.HBM),
        pltpu.with_memory_space_constraint(counts.transpose(0, 2, 3, 1), pltpu.HBM),
        pltpu.with_memory_space_constraint(jnp.asarray(constants()), pltpu.HBM),
    )
    kept, arrivals = pl.pallas_call(
        finish,
        out_shape=shapes,
        in_specs=[in_vmem, in_vmem, in_vmem],
        out_specs=(in_vmem, in_vmem),
        name="finish",
    )(*(pltpu.with_memory_space_constraint(result, pltpu.VMEM) for result in results))
    return kept.reshape(2, 5, 1, ROWS * 128), arrivals.reshape(2, 5, 1, 2 * BLOCK * 128)


def solution(mesh):
    return jax.shard_map(
        functools.partial(local, mesh.shape["cuts"]),
        mesh=mesh,
        in_specs=(
            P(None, None, "cuts", "dom"),
            P(None, "cuts", "dom"),
            P(None, None, "cuts", "dom"),
        ),
        out_specs=(P(None, None, "cuts", "dom"), P(None, None, "cuts", "dom")),
        check_vma=False,
    )
```
